32 devices in a mesh: trade: 8 (over z, y), factor: 4 (over x, core).
Axes of the slice: x: 2, y: 2, z: 4, core: 2. Of those that a mesh axis runs over, the one named last changes fastest.
Arguments:
- sensitivity: bfloat16 [32768, 6400], P('trade', 'factor'), may hold values from -6 to 6
- block_count: int32 [64], P('trade'), may hold values from 0 to 512, as said below
- trade_node: int32 [32768], P('trade'), may hold values from 0 to 4095
- factor_bucket: int32 [6400], replicated, may hold values from 0 to 17, as said below
- risk_weight: float32 [18], replicated, may hold values from 0.005 to 0.12
- bucket_loading: float32 [18], replicated, may hold values from 0.5 to 1
Outputs:
- capital_scaled: float32 [3], replicated
- trade_alloc: float32 [3, 32768], P(None, ('trade', 'factor'))
- node_alloc: float32 [3, 18, 4096], P(None, None, ('trade', 'factor'))
The draws below stay inside these ranges and needn't reach their ends.
Inputs may be any that keep to these rules, and one draw needn't show every extreme that they name: `block_count`: every index of trade either has all its 8 blocks full (512) or every block of it holds at most 128 trades; at least one index is full. `factor_bucket`: the 5 factors of a name share a bucket; each bucket holds 71 names or one more.
All inputs are finite; a program needn't handle non-finite values.
Results may differ from the reference program's by a relative error of at most 0.007.
Values sent between devices are 32-bit elements; how exact they have to be, the bound alone decides.
No kernel may reach another device: no remote copies, remote signals or barrier semaphores. Data moves between devices by JAX's collectives and lax.ppermute only.
A program may use at most 64 MiB of HBM per device.

```python
import math
import jax
import jax.numpy as jnp
from jax import lax

NAMES = 1280
TENORS = 5
BUCKETS = 18
SCEN = 3
NODES = 4096
BLOCKS_DEV = 8
BLOCK = 512
F = 6400
BLOCKS = 64
TRADES = 32768


def draw_block_count(key, part):
    keys = jax.random.split(key, 4)
    groups = BLOCKS // BLOCKS_DEV
    heavy = jax.random.randint(keys[0], (groups,), 0, 4)
    chosen = jax.random.randint(keys[1], (), 0, groups)
    heavy = jnp.where(jnp.arange(groups) == chosen, 0, heavy)
    light = jax.random.randint(keys[2], (BLOCKS,), 1, BLOCK // 4 + 1)
    coin = jax.random.randint(keys[3], (BLOCKS,), 0, 2)
    full = jnp.repeat(heavy == 0, BLOCKS_DEV)
    return jnp.where(full, BLOCK, light * coin).astype(jnp.int32)


def draw_factor_bucket(key, part):
    order = jax.random.permutation(key, NAMES)
    buckets = (order % BUCKETS).astype(jnp.int32)
    return jnp.repeat(buckets, TENORS).astype(jnp.int32)


def set_ends(values, own_key, low, high):
    extent = values.shape
    spot = [jax.random.randint(jax.random.fold_in(own_key, axis), (), 0, extent[axis]) for axis in range(len(extent))]
    values = values.at[tuple(spot)].set(low)
    longest = extent.index(max(extent))
    spot[longest] = (spot[longest] + 1) % extent[longest]
    return values.at[tuple(spot)].set(high)


def steps_of(key, shape, pieces, low, largest):
    loudness = 1.0
    for axis_at, shards_of in pieces:
        heights = jax.random.uniform(jax.random.fold_in(jax.random.fold_in(key, 6), axis_at), (shards_of,), jnp.float32, low / len(pieces), largest / len(pieces))
        loudness = loudness * jnp.repeat(jnp.exp(heights), shape[axis_at] // shards_of).reshape((-1,) + (1,) * (len(shape) - 1 - axis_at))
    return loudness


def normal_values(stream_key, shape, deviation, limit, cuts=(), kind=jnp.bfloat16):
    values = jax.random.normal(stream_key, shape, jnp.float32) * deviation
    if len(cuts) > 0:
        values = steps_of(stream_key, shape, cuts, -0.22, 0.18) * values
    return jnp.clip(values, min=-limit, max=limit).astype(kind)


def setup_inputs(seed: int = 0) -> dict:
    seeds = jax.random.split(jax.random.key(seed), 7)
    return {
        "sensitivity": normal_values(seeds[0], (TRADES, F), 1.0, 6.0, ((0, 8), (1, 4))),
        "block_count": draw_block_count(jax.random.fold_in(seeds[6], 71), 0),
        "trade_node": set_ends(jax.random.randint(seeds[2], (TRADES,), 0, NODES), jax.random.fold_in(seeds[2], 1), 0, NODES - 1).astype(jnp.int32),
        "factor_bucket": draw_factor_bucket(jax.random.fold_in(seeds[6], 71), 0),
        "risk_weight": jnp.clip(jnp.exp(jax.random.uniform(seeds[4], (BUCKETS,), jnp.float32, math.log(0.005), math.log(0.12))), 0.005, 0.12),
        "bucket_loading": jnp.clip(jax.random.uniform(seeds[5], (BUCKETS,), jnp.float32, 0.5, 1.0), 0.5, 1.0),
    }


cross_base = 0.5

def level_table():
    base = jnp.array([1.0, 0.65, 0.35, 0.2275], dtype=jnp.float32)
    return jnp.stack([base, jnp.minimum(1.25 * base, 1.0), jnp.maximum(2.0 * base - 1.0, 0.75 * base)])

def correlated(weighted, name_bucket, first_name, count):
    grid = weighted.reshape(-1, TENORS)
    names_onehot = (jnp.arange(BUCKETS, dtype=jnp.int32)[:, None] == name_bucket[None, :]).astype(jnp.float32)
    tenor_sums = jnp.dot(names_onehot, grid, precision=lax.Precision.HIGHEST)
    name_sums = lax.optimization_barrier(jnp.sum(grid, 1))
    bucket_total = lax.optimization_barrier(jnp.sum(tenor_sums, 1))
    own_grid = lax.dynamic_slice_in_dim(grid, first_name, count, 0)
    own_onehot = lax.dynamic_slice_in_dim(names_onehot, first_name, count, 1)
    own_tenor = jnp.dot(own_onehot.T, tenor_sums, precision=lax.Precision.HIGHEST)
    own_total = jnp.dot(own_onehot.T, bucket_total, precision=lax.Precision.HIGHEST)
    own_name = lax.dynamic_slice_in_dim(name_sums, first_name, count, 0)
    levels = level_table()
    same_both = (levels[:, 0] - levels[:, 1] - levels[:, 2] + levels[:, 3])[:, None, None]
    product = levels[:, 3, None, None] * own_total[None, :, None]
    product = product + (levels[:, 2] - levels[:, 3])[:, None, None] * own_tenor[None, :, :]
    product = product + (levels[:, 1] - levels[:, 3])[:, None, None] * own_name[None, :, None]
    product = product + same_both * own_grid[None, :, :]
    return product.reshape(SCEN, count * TENORS)

def capital_terms(bucket_forms, bucket_sums, loading):
    scenario = jnp.array([1.0, 1.25, 0.75], dtype=jnp.float32)[:, None]
    root_forms = jnp.sqrt(bucket_forms + 1e-06)
    radius = jnp.sqrt(root_forms * root_forms + bucket_sums[None, :] * bucket_sums[None, :])
    capped = bucket_sums[None, :] * root_forms / radius
    loaded = lax.optimization_barrier(jnp.sum(loading[None, :] * capped, 1, keepdims=True))
    squares = lax.optimization_barrier(jnp.sum((loading[None, :] * capped) ** 2, 1, keepdims=True))
    cross_term = cross_base * scenario * (loaded * loaded - squares)
    total_form = lax.optimization_barrier(jnp.sum(root_forms * root_forms, 1, keepdims=True)) + cross_term
    capital = jnp.sqrt(total_form)
    cross_pull = cross_base * scenario * (loading[None, :] * loaded - loading[None, :] ** 2 * capped) / capital
    grad_root = root_forms / capital + cross_pull * (bucket_sums[None, :] / radius) ** 3
    coef_form = grad_root / root_forms
    coef_sum = cross_pull * (root_forms / radius) ** 3
    return (capital[:, 0], coef_form, coef_sum)

def reference(sensitivity, block_count, trade_node, factor_bucket, risk_weight, bucket_loading):
    factors = sensitivity.shape[1]
    slot_index = jnp.arange(BLOCK, dtype=jnp.int32)
    live_mask = (slot_index[None, :] < block_count[:, None]).astype(jnp.float32)
    live_flat = live_mask.reshape(-1)
    raw_totals = jnp.dot(live_flat.astype(jnp.bfloat16)[None, :], sensitivity, preferred_element_type=jnp.float32)[0]
    onehot = (jnp.arange(BUCKETS, dtype=jnp.int32)[:, None] == factor_bucket[None, :]).astype(jnp.float32)
    factor_weight = lax.optimization_barrier(jnp.sum(onehot * risk_weight[:, None], 0))
    weighted = factor_weight * raw_totals
    name_bucket = factor_bucket.reshape(-1, TENORS)[:, 0]
    products = correlated(weighted, name_bucket, 0, factors // TENORS)
    bucket_forms = jnp.dot(products * weighted[None, :], onehot.T, precision=lax.Precision.HIGHEST)
    bucket_sums = jnp.dot(onehot, weighted, precision=lax.Precision.HIGHEST)
    capital, coef_form, coef_sum = capital_terms(bucket_forms, bucket_sums, bucket_loading)
    gradient = factor_weight[None, :] * (products * jnp.dot(coef_form, onehot, precision=lax.Precision.HIGHEST) + jnp.dot(coef_sum, onehot, precision=lax.Precision.HIGHEST))
    spread = (gradient[:, None, :] * onehot[None, :, :]).reshape(SCEN * BUCKETS, factors).astype(jnp.bfloat16)
    blocked = sensitivity.reshape(BLOCKS, BLOCK, factors)

    def one_block(inputs_pair):
        piece_sens, piece_mask = inputs_pair
        product_block = lax.dot_general(spread, piece_sens, (((1,), (1,)), ((), ())), preferred_element_type=jnp.float32)
        return product_block * piece_mask[None, :]
    alloc = lax.map(one_block, (blocked, live_mask)).transpose(1, 0, 2).reshape(SCEN * BUCKETS, TRADES)
    trade_alloc = alloc.reshape(SCEN, BUCKETS, TRADES).sum(1) * (TRADES / capital)[:, None]
    node_sums = jax.ops.segment_sum(alloc.T, trade_node, num_segments=NODES).T
    node_alloc = node_sums.reshape(SCEN, BUCKETS, NODES) * (NODES / capital)[:, None, None]
    capital_scaled = capital / TRADES ** 0.5
    return (capital_scaled, trade_alloc, node_alloc)
```

```python
import functools

import jax
import jax.numpy as jnp
import numpy as np
from jax import lax
from jax.experimental import pallas as pl
from jax.experimental.pallas import tpu as pltpu
from jax.sharding import PartitionSpec as P

TENORS = 5
BUCKETS = 18
SCEN = 3
NODES = 4096
BLOCK = 512
ROWS = 3 * BUCKETS
LOW = 256
HIGH = NODES // LOW
AXES = ("trade", "factor")
MIB = 1 << 20

BASE = np.array([1.0, 0.65, 0.35, 0.2275], np.float32)
LEVELS = np.stack([BASE, np.minimum(1.25 * BASE, 1.0), np.maximum(2.0 * BASE - 1.0, 0.75 * BASE)])
SCENARIO = (1.0, 1.25, 0.75)
CROSS = 0.5
SAME_BOTH = LEVELS[:, 0] - LEVELS[:, 1] - LEVELS[:, 2] + LEVELS[:, 3]

SMEM = pl.BlockSpec(memory_space=pltpu.SMEM)
VMEM = pl.BlockSpec(memory_space=pltpu.VMEM)
ANY = pl.BlockSpec(memory_space=pl.ANY)
f32 = jnp.float32
bf16 = jnp.bfloat16


def shape(*dims, dtype=f32):
    return jax.ShapeDtypeStruct(dims, dtype)


def call(kernel, out_shape, in_specs, out_specs, name, scratch=(), flops=0, limit=24):
    return pl.pallas_call(
        kernel,
        out_shape=out_shape,
        in_specs=in_specs,
        out_specs=out_specs,
        scratch_shapes=list(scratch),
        name=name,
        compiler_params=pltpu.CompilerParams(vmem_limit_bytes=limit * MIB),
        cost_estimate=pl.CostEstimate(flops=flops, bytes_accessed=1 << 16, transcendentals=0),
    )


def dot_t(a, b):
    return lax.dot_general(a, b, (((1,), (1,)), ((), ())), preferred_element_type=f32)


def totals_kernel(count, sens, held, raw, sems):
    blocks = count.shape[0]
    width = sens.shape[1]
    copies = []
    for i in range(blocks):
        part = pl.ds(i * BLOCK, BLOCK)
        copies.append(pltpu.make_async_copy(sens.at[part], held.at[part], sems.at[i]))
        copies[-1].start()
    row = lax.broadcasted_iota(jnp.int32, (16, width), 0)
    total = jnp.zeros((16, width), f32)
    for i in range(blocks):
        copies[i].wait()
        live = count[i]

        def step(g, total):
            part = held[pl.ds(pl.multiple_of(i * BLOCK + g * 16, 16), 16), :].astype(f32)
            return total + jnp.where(row < live - g * 16, part, 0.0)

        total = lax.fori_loop(0, BLOCK // 16, step, total, unroll=4)
    raw[...] = jnp.sum(total, 0, keepdims=True)


def tables_kernel(
    me,
    weight,
    nodes,
    bucket,
    tenor,
    low_hot,
    high_hot,
    spread_hot,
    tenor_hot,
    factor_weight,
    *,
    spots,
):
    bits = len(spots[0])
    inner = (NODES >> bits).bit_length() - 1
    node = nodes[...]
    owner = node >> inner
    other = owner ^ me[0]
    label = node & ((1 << inner) - 1)
    for i in range(bits):
        spot = jnp.where((owner & 1) == 0, spots[0][i], spots[1][i])
        label = label + ((other >> i) & 1) * spot
    low = label & (LOW - 1)
    high = label >> (LOW.bit_length() - 1)
    trades = node.shape[1]
    for start in range(0, trades, 512):
        part = pl.ds(start, 512)
        here = lax.broadcasted_iota(jnp.int32, (LOW, 512), 0) == low[:, start : start + 512]
        low_hot[:, part] = jnp.where(here, 1.0, 0.0).astype(bf16)
        here = lax.broadcasted_iota(jnp.int32, (HIGH, 512), 0) == high[:, start : start + 512]
        high_hot[:, part] = jnp.where(here, 1.0, 0.0).astype(bf16)
    own = bucket[...]
    width = own.shape[1]
    row = lax.broadcasted_iota(jnp.int32, (56, width), 0)
    hit = (row == own) | (row == own + BUCKETS) | (row == own + 2 * BUCKETS)
    spread_hot[...] = jnp.where(hit, 1.0, 0.0)
    row = lax.broadcasted_iota(jnp.int32, (24, width), 0)
    for m in range(TENORS):
        tenor_hot[24 * m : 24 * m + 24, :] = jnp.where(
            (row == own) & (tenor[...] == m), 1.0, 0.0
        )
    total = jnp.zeros((1, width), f32)
    for b in range(BUCKETS):
        total = jnp.where(own == b, weight[b], total)
    factor_weight[...] = total


def weights_kernel(first, second, factor_weight, tenor, spread_hot, tenor_hot, spread, sums):
    width = first.shape[1]
    weighted = factor_weight[...] * (first[...] + second[...])
    own_tenor = tenor[...]
    name = weighted
    for d in range(1, TENORS):
        zeros = jnp.zeros((1, d), f32)
        after = jnp.concatenate([weighted[:, d:], zeros], 1)
        before = jnp.concatenate([zeros, weighted[:, : width - d]], 1)
        name = name + jnp.where(own_tenor < TENORS - d, after, 0.0)
        name = name + jnp.where(own_tenor >= d, before, 0.0)
    near = float(LEVELS[0, 1] - LEVELS[0, 3]) * name + float(SAME_BOTH[0]) * weighted
    row = lax.broadcasted_iota(jnp.int32, (56, width), 0)
    value = jnp.where(row < BUCKETS, near, jnp.where(row < 2 * BUCKETS, weighted, 1.0))
    full = spread_hot[...] * value
    upper = full.astype(bf16)
    lower = (full[:40] - upper[:40].astype(f32)).astype(bf16)
    spread[...] = jnp.concatenate(
        [upper.astype(f32), tenor_hot[...], lower.astype(f32)], 0
    ).astype(bf16)
    lane = lax.broadcasted_iota(jnp.int32, (24, 128), 1)
    out = jnp.zeros((24, 128), f32)
    square = jnp.zeros((24, 1), f32)
    for m in range(TENORS):
        hot = tenor_hot[24 * m : 24 * m + 24, :]
        part = hot * weighted
        out = jnp.where(lane == m, jnp.sum(part, 1, keepdims=True), out)
        square = square + jnp.sum(part * weighted, 1, keepdims=True)
        if m == 0:
            names = jnp.sum(hot * (name * name), 1, keepdims=True)
    out = jnp.where(lane == TENORS, square, out)
    out = jnp.where(lane == TENORS + 1, names, out)
    sums[...] = out


def spread_kernel(spread, held, near, tenors):
    trades = held.shape[0]
    for start in range(0, trades, BLOCK):
        part = pl.ds(start, BLOCK)
        out = dot_t(spread[...], held[part, :])
        near[:, part] = jnp.concatenate([out[:40] + out[176:216], out[40:56]], 0)
        tenors[:, part] = out[56:176]


def nodes_kernel(
    count, sums, more, near, tenors, low_hot, high_hot, alloc, total, keep, send, rounded
):
    trades = near.shape[1]
    gather = sums[...] + more[...]
    total[...] = gather
    lane = lax.broadcasted_iota(jnp.int32, (24, 128), 1)
    bucket = jnp.sum(jnp.where(lane < TENORS, gather, 0.0), 1, keepdims=True)
    pull = [
        float(LEVELS[0, 2] - LEVELS[0, 3]) * gather[:, m : m + 1] + float(LEVELS[0, 3]) * bucket
        for m in range(TENORS)
    ]
    slot = lax.broadcasted_iota(jnp.int32, (1, BLOCK), 1)
    for i in range(trades // BLOCK):
        part = pl.ds(i * BLOCK, BLOCK)
        live = jnp.where(slot < count[i], 1.0, 0.0)
        far = near[:24, part]
        for m in range(TENORS):
            far = far + pull[m] * tenors[24 * m : 24 * m + 24, part]
        value = jnp.concatenate([far, near[24:, part]], 0) * live
        alloc[:, part] = value
        rounded[:, part] = jnp.concatenate([value, jnp.zeros((8, BLOCK), f32)], 0).astype(bf16)
    step = 4
    for h in range(0, HIGH, step):
        value = rounded[...]
        masked = jnp.concatenate([value * high_hot[h + j : h + j + 1, :] for j in range(step)], 0)
        out = dot_t(masked, low_hot[...])
        for j in range(step):
            keep[h + j] = out[64 * j : 64 * j + ROWS, : LOW // 2]
            send[h + j] = out[64 * j : 64 * j + ROWS, LOW // 2 :]


def capital_kernel(place, terms, total, alloc, keep, send, mix, capital, *, trades_total):
    parts = 2 * keep.shape[0]
    length = keep.shape[2]
    gather = total[...]
    lane = lax.broadcasted_iota(jnp.int32, (24, 128), 1)
    real = lax.broadcasted_iota(jnp.int32, (24, 1), 0) < BUCKETS
    risk = terms[:, 0:1]
    loading = terms[:, 1:2]
    tenor_part = jnp.where(lane < TENORS, gather, 0.0)
    sums = jnp.sum(tenor_part, 1, keepdims=True)
    tenor_square = jnp.sum(tenor_part * tenor_part, 1, keepdims=True)
    own_square = gather[:, TENORS : TENORS + 1]
    name_square = gather[:, TENORS + 1 : TENORS + 2]
    columns = []
    row8 = lax.broadcasted_iota(jnp.int32, (8, 128), 0)
    capitals = jnp.zeros((8, 128), f32)
    for s in range(SCEN):
        level = [float(v) for v in LEVELS[s]]
        form = level[3] * sums * sums + (level[2] - level[3]) * tenor_square
        form = form + (level[1] - level[3]) * name_square + float(SAME_BOTH[s]) * own_square
        root = jnp.sqrt(form + 1e-6)
        radius = jnp.sqrt(root * root + sums * sums)
        capped = sums * root / radius
        pulled = jnp.where(real, loading * capped, 0.0)
        loaded = jnp.sum(pulled, 0, keepdims=True)
        squares = jnp.sum(pulled * pulled, 0, keepdims=True)
        cross = CROSS * SCENARIO[s]
        inside = jnp.sum(jnp.where(real, root * root, 0.0), 0, keepdims=True)
        cap = jnp.sqrt(inside + cross * (loaded * loaded - squares))
        cross_pull = cross * (loading * loaded - loading * loading * capped) / cap
        ratio = sums / radius
        share = root / radius
        coef_form = (root / cap + cross_pull * ratio * ratio * ratio) / root
        coef_sum = cross_pull * share * share * share
        scale = risk / cap
        columns.append(
            [
                (scale * coef_form * SCENARIO[s])[:BUCKETS],
                (scale * coef_form * (1.0 - SCENARIO[s]))[:BUCKETS],
                (scale * coef_sum)[:BUCKETS],
            ]
        )
        capitals = jnp.where(row8 == s, cap, capitals)
    capital[...] = capitals
    column = []
    for s in range(SCEN):
        column.append(jnp.concatenate(columns[s] + [jnp.zeros((2, 1), f32)], 0))
        mix[s] = jnp.broadcast_to(column[s][:ROWS] * float(NODES), (ROWS, 128))
    for p in range(parts):
        block = place[p]
        rows = pl.ds(pl.multiple_of(block * length, 128), length)
        value = alloc[:, rows]
        out = jnp.concatenate(
            [jnp.sum(value * (column[s] * float(trades_total)), 0, keepdims=True) for s in range(SCEN)],
            0,
        )
        if p < parts // 2:
            keep[p] = out
        else:
            send[p - parts // 2] = out


def bit_reverse(value, bits):
    return sum(((value >> i) & 1) << (bits - 1 - i) for i in range(bits))


def local(
    sensitivity,
    block_count,
    trade_node,
    factor_bucket,
    risk_weight,
    bucket_loading,
    *,
    trade_size,
    factor_size,
):
    trade_rows, width = sensitivity.shape
    trades_total = trade_rows * trade_size
    devices = trade_size * factor_size
    trade_bits = trade_size.bit_length() - 1
    factor_bits = factor_size.bit_length() - 1
    bits = trade_bits + factor_bits
    inner = (NODES // devices).bit_length() - 1
    t = lax.axis_index("trade")
    f = lax.axis_index("factor")
    me = t * factor_size + f

    def exchange(x, bit_of):
        pairs = [(o, o ^ (1 << bit_of(o))) for o in range(devices)]
        return lax.ppermute(x, AXES, pairs)

    upper_f = list(range(1, factor_bits))
    all_t = list(range(factor_bits, bits))
    orders = [upper_f + all_t, all_t[:2] + upper_f + all_t[2:]]
    places = [7, 11, 10, 9, 8, 6, 5, 4, 3, 2, 1, 0]
    spots = [[0] * bits, [0] * bits]
    for c in range(2):
        for i, bit in enumerate([0] + orders[c]):
            spots[c][bit] = 1 << places[i]
    block_order = jnp.array(
        [bit_reverse(p, factor_bits) for p in range(factor_size)], jnp.int32
    ) ^ f.astype(jnp.int32)
    bucket = lax.dynamic_slice_in_dim(factor_bucket, f * width, width, 0)[None, :]
    tenor = (jnp.arange(width, dtype=jnp.int32) % TENORS)[None, :]
    terms = jnp.zeros((24, 128), f32)
    terms = terms.at[:BUCKETS, 0].set(risk_weight).at[:BUCKETS, 1].set(bucket_loading)

    held, raw = call(
        totals_kernel,
        (pltpu.VMEM(sensitivity.shape, bf16), shape(1, width)),
        [SMEM, ANY],
        (VMEM, VMEM),
        "totals",
        scratch=[pltpu.SemaphoreType.DMA((block_count.shape[0],))],
        flops=10**7,
    )(block_count, sensitivity)

    low_hot, high_hot, spread_hot, tenor_hot, factor_weight = call(
        functools.partial(tables_kernel, spots=spots),
        (
            pltpu.VMEM((LOW, trade_rows), bf16),
            pltpu.VMEM((HIGH, trade_rows), bf16),
            pltpu.VMEM((56, width), f32),
            pltpu.VMEM((24 * TENORS, width), f32),
            pltpu.VMEM((1, width), f32),
        ),
        [SMEM, SMEM, VMEM, VMEM, VMEM],
        (VMEM,) * 5,
        "tables",
        flops=10**7,
    )(me.astype(jnp.int32)[None], risk_weight, trade_node[None, :], bucket, tenor)

    other = None
    for i in range(trade_bits):
        if other is not None:
            raw = raw + other
        other = exchange(raw, lambda o, i=i: factor_bits + i)

    spread, sums = call(
        weights_kernel,
        (pltpu.VMEM((216, width), bf16), shape(24, 128)),
        [VMEM] * 6,
        (VMEM, VMEM),
        "weights",
        flops=10**6,
    )(raw, other, factor_weight, tenor, spread_hot, tenor_hot)

    near, tenors = call(
        spread_kernel,
        (pltpu.VMEM((56, trade_rows), f32), pltpu.VMEM((24 * TENORS, trade_rows), f32)),
        [VMEM, VMEM],
        (VMEM, VMEM),
        "spread",
        flops=2 * 216 * width * trade_rows,
    )(spread, held)

    more = None
    for i in range(factor_bits):
        if more is not None:
            sums = sums + more
        more = exchange(sums, lambda o, i=i: i)

    alloc, total, keep, send = call(
        nodes_kernel,
        (
            pltpu.VMEM((56, trade_rows), f32),
            shape(24, 128),
            shape(HIGH, ROWS, LOW // 2),
            shape(HIGH, ROWS, LOW // 2),
        ),
        [SMEM, VMEM, VMEM, VMEM, VMEM, VMEM, VMEM],
        (VMEM,) * 4,
        "nodes",
        scratch=[pltpu.VMEM((64, trade_rows), bf16)],
        flops=2 * 1024 * trade_rows * LOW,
        limit=40,
    )(block_count, sums, more, near, tenors, low_hot, high_hot)

    length = trade_rows // factor_size
    trade_keep, trade_send, mix, capital = call(
        functools.partial(capital_kernel, trades_total=trades_total),
        (
            shape(factor_size // 2, SCEN, length),
            shape(factor_size // 2, SCEN, length),
            shape(SCEN, ROWS, 128),
            shape(8, 128),
        ),
        [SMEM, VMEM, VMEM, VMEM],
        (VMEM,) * 4,
        "capital",
        flops=10**7,
    )(block_order, terms, total, alloc)

    keep = keep + exchange(send, lambda o: 0)
    for i in range(bits - 1):
        if keep.shape[0] > 1:
            half = keep.shape[0] // 2
            send, keep = keep[half:], keep[:half]
        else:
            half = keep.shape[2] // 2
            send, keep = keep[..., half:], keep[..., :half]
        keep = keep + exchange(send, lambda o, i=i: orders[o & 1][i])
    keep = keep[0]

    trade_keep = trade_keep + exchange(trade_send, lambda o: 0)
    for i in range(1, factor_bits):
        half = trade_keep.shape[0] // 2
        trade_send, trade_keep = trade_keep[half:], trade_keep[:half]
        trade_keep = trade_keep + exchange(trade_send, lambda o, i=i: i)

    mixed = mix[:, :, : keep.shape[1]] * keep[None]
    node_alloc = mixed.reshape(SCEN, 3, BUCKETS, keep.shape[1]).sum(1)
    capital_scaled = capital[:SCEN, 0] / trades_total**0.5
    return (capital_scaled, trade_keep[0], node_alloc)


def solution(mesh):
    sizes = dict(mesh.shape)
    return jax.shard_map(
        functools.partial(local, trade_size=sizes["trade"], factor_size=sizes["factor"]),
        mesh=mesh,
        in_specs=(P("trade", "factor"), P("trade"), P("trade"), P(), P(), P()),
        out_specs=(P(), P(None, ("trade", "factor")), P(None, None, ("trade", "factor"))),
        check_vma=False,
    )
```

```python
import functools

import jax
import jax.numpy as jnp
import numpy as np
from jax import lax
from jax.experimental import pallas as pl
from jax.experimental.pallas import tpu as pltpu
from jax.sharding import PartitionSpec as P

TENORS = 5
BUCKETS = 18
SCEN = 3
NODES = 4096
BLOCK = 512
ROWS = 3 * BUCKETS
PIECE = 160
LOW = 256
HIGH = NODES // LOW
AXES = ("trade", "factor")
MIB = 1 << 20

BASE = np.array([1.0, 0.65, 0.35, 0.2275], np.float32)
LEVELS = np.stack([BASE, np.minimum(1.25 * BASE, 1.0), np.maximum(2.0 * BASE - 1.0, 0.75 * BASE)])
SCENARIO = (1.0, 1.25, 0.75)
CROSS = 0.5
SAME_BOTH = LEVELS[:, 0] - LEVELS[:, 1] - LEVELS[:, 2] + LEVELS[:, 3]

SMEM = pl.BlockSpec(memory_space=pltpu.SMEM)
VMEM = pl.BlockSpec(memory_space=pltpu.VMEM)
ANY = pl.BlockSpec(memory_space=pl.ANY)
f32 = jnp.float32
bf16 = jnp.bfloat16


def shape(*dims, dtype=f32):
    return jax.ShapeDtypeStruct(dims, dtype)


def call(kernel, out_shape, in_specs, out_specs, name, scratch=(), flops=0, limit=12):
    return pl.pallas_call(
        kernel,
        out_shape=out_shape,
        in_specs=in_specs,
        out_specs=out_specs,
        scratch_shapes=list(scratch),
        name=name,
        compiler_params=pltpu.CompilerParams(vmem_limit_bytes=limit * MIB),
        cost_estimate=pl.CostEstimate(flops=flops, bytes_accessed=1 << 16, transcendentals=0),
    )


def dot(a, b):
    return lax.dot_general(a, b, (((1,), (0,)), ((), ())), preferred_element_type=f32)


def dot_t(a, b):
    return lax.dot_general(a, b, (((1,), (1,)), ((), ())), preferred_element_type=f32)


def totals_kernel(count, sens, held, raw, partial, sems):
    width, trades = sens.shape
    pieces = width // PIECE
    lanes = 128

    def copy(i):
        part = pl.ds(pl.multiple_of(i * PIECE, PIECE), PIECE)
        return pltpu.make_async_copy(sens.at[part], held.at[part], sems.at[i])

    for i in range(pieces):
        copy(i).start()

    def run(tiles):
        def piece(i, carry):
            copy(i).wait()
            rows = pl.ds(pl.multiple_of(i * PIECE, PIECE), PIECE)
            total = jnp.zeros((PIECE, lanes), f32)
            for start, live in tiles:
                part = held[rows, start : start + lanes].astype(f32)
                total = total + (part if live is None else jnp.where(live, part, 0.0))
            partial[rows, :] = total
            return carry

        lax.fori_loop(0, pieces, piece, 0)

    full = count[0] == BLOCK

    @pl.when(full)
    def _():
        run([(start, None) for start in range(0, trades, lanes)])

    @pl.when(jnp.logical_not(full))
    def _():
        slot = lax.broadcasted_iota(jnp.int32, (PIECE, lanes), 1)
        run([(i * BLOCK, slot < count[i]) for i in range(trades // BLOCK)])

    value = partial[...]
    upper = value.astype(bf16)
    value = value - upper.astype(f32)
    middle = value.astype(bf16)
    lower = (value - middle.astype(f32)).astype(bf16)
    ones = jnp.ones((16, 3 * lanes), bf16)
    raw[...] = dot_t(ones, jnp.concatenate([upper, middle, lower], 1))[:1]


def tables_kernel(
    me,
    weight,
    nodes,
    bucket,
    tenor,
    low_hot,
    high_hot,
    spread_hot,
    tenor_hot,
    factor_weight,
    *,
    spots,
):
    bits = len(spots[0])
    inner = (NODES >> bits).bit_length() - 1
    node = nodes[...]
    owner = node >> inner
    other = owner ^ me[0]
    label = node & ((1 << inner) - 1)
    for i in range(bits):
        spot = jnp.where((owner & 1) == 0, spots[0][i], spots[1][i])
        label = label + ((other >> i) & 1) * spot
    low = label & (LOW - 1)
    high = label >> (LOW.bit_length() - 1)
    trades = node.shape[1]
    for start in range(0, trades, 512):
        part = pl.ds(start, 512)
        here = lax.broadcasted_iota(jnp.int32, (LOW, 512), 0) == low[:, start : start + 512]
        low_hot[:, part] = jnp.where(here, 1.0, 0.0).astype(bf16)
        here = lax.broadcasted_iota(jnp.int32, (HIGH, 512), 0) == high[:, start : start + 512]
        high_hot[:, part] = jnp.where(here, 1.0, 0.0).astype(bf16)
    own = bucket[...]
    width = own.shape[1]
    row = lax.broadcasted_iota(jnp.int32, (56, width), 0)
    hit = (row == own) | (row == own + BUCKETS) | (row == own + 2 * BUCKETS)
    spread_hot[...] = jnp.where(hit, 1.0, 0.0)
    row = lax.broadcasted_iota(jnp.int32, (24, width), 0)
    for m in range(TENORS):
        tenor_hot[24 * m : 24 * m + 24, :] = jnp.where(
            (row == own) & (tenor[...] == m), 1.0, 0.0
        )
    total = jnp.zeros((1, width), f32)
    for b in range(BUCKETS):
        total = jnp.where(own == b, weight[b], total)
    factor_weight[...] = total


def weights_kernel(first, second, factor_weight, tenor, spread_hot, tenor_hot, spread, sums):
    width = first.shape[1]
    weighted = factor_weight[...] * (first[...] + second[...])
    own_tenor = tenor[...]
    name = weighted
    for d in range(1, TENORS):
        zeros = jnp.zeros((1, d), f32)
        after = jnp.concatenate([weighted[:, d:], zeros], 1)
        before = jnp.concatenate([zeros, weighted[:, : width - d]], 1)
        name = name + jnp.where(own_tenor < TENORS - d, after, 0.0)
        name = name + jnp.where(own_tenor >= d, before, 0.0)
    near = float(LEVELS[0, 1] - LEVELS[0, 3]) * name + float(SAME_BOTH[0]) * weighted
    row = lax.broadcasted_iota(jnp.int32, (56, width), 0)
    value = jnp.where(row < BUCKETS, near, jnp.where(row < 2 * BUCKETS, weighted, 1.0))
    full = spread_hot[...] * value
    upper = full.astype(bf16)
    lower = full[:40] - upper[:40].astype(f32)
    fill = jnp.zeros((32, width), f32)
    spread[...] = jnp.concatenate([upper.astype(f32), lower, fill], 0).astype(bf16)
    lane = lax.broadcasted_iota(jnp.int32, (24, 128), 1)
    out = jnp.zeros((24, 128), f32)
    square = jnp.zeros((24, 1), f32)
    for m in range(TENORS):
        hot = tenor_hot[24 * m : 24 * m + 24, :]
        part = hot * weighted
        out = jnp.where(lane == m, jnp.sum(part, 1, keepdims=True), out)
        square = square + jnp.sum(part * weighted, 1, keepdims=True)
        if m == 0:
            names = jnp.sum(hot * (name * name), 1, keepdims=True)
    out = jnp.where(lane == TENORS, square, out)
    out = jnp.where(lane == TENORS + 1, names, out)
    sums[...] = out


def ones_kernel(tenor_hot, held, tenors):
    trades = held.shape[1]
    hot = jnp.concatenate([tenor_hot[...], jnp.zeros((8, held.shape[0]), f32)], 0).astype(bf16)
    for start in range(0, trades, BLOCK):
        part = pl.ds(start, BLOCK)
        tenors[:, part] = dot(hot, held[:, part])[: 24 * TENORS]


def spread_kernel(spread, held, near):
    trades = held.shape[1]
    for start in range(0, trades, BLOCK):
        part = pl.ds(start, BLOCK)
        out = dot(spread[...], held[:, part])
        near[:, part] = jnp.concatenate([out[:40] + out[56:96], out[40:56]], 0)


def nodes_kernel(
    count, sums, more, near, tenors, low_hot, high_hot, alloc, total, keep, send, rounded
):
    trades = near.shape[1]
    gather = sums[...] + more[...]
    total[...] = gather
    lane = lax.broadcasted_iota(jnp.int32, (24, 128), 1)
    bucket = jnp.sum(jnp.where(lane < TENORS, gather, 0.0), 1, keepdims=True)
    pull = [
        float(LEVELS[0, 2] - LEVELS[0, 3]) * gather[:, m : m + 1] + float(LEVELS[0, 3]) * bucket
        for m in range(TENORS)
    ]
    slot = lax.broadcasted_iota(jnp.int32, (1, BLOCK), 1)
    for i in range(trades // BLOCK):
        part = pl.ds(i * BLOCK, BLOCK)
        live = jnp.where(slot < count[i], 1.0, 0.0)
        far = near[:24, part]
        for m in range(TENORS):
            far = far + pull[m] * tenors[24 * m : 24 * m + 24, part]
        value = jnp.concatenate([far, near[24:, part]], 0) * live
        alloc[:, part] = value
        rounded[:, part] = jnp.concatenate([value, jnp.zeros((8, BLOCK), f32)], 0).astype(bf16)
    step = 4
    for h in range(0, HIGH, step):
        value = rounded[...]
        masked = jnp.concatenate([value * high_hot[h + j : h + j + 1, :] for j in range(step)], 0)
        out = dot_t(masked, low_hot[...])
        for j in range(step):
            keep[h + j] = out[64 * j : 64 * j + ROWS, : LOW // 2]
            send[h + j] = out[64 * j : 64 * j + ROWS, LOW // 2 :]


def capital_kernel(place, weight, load, total, alloc, keep, send, mix, capital, *, trades_total):
    parts = 2 * keep.shape[0]
    length = keep.shape[2]
    gather = total[...]
    lane = lax.broadcasted_iota(jnp.int32, (24, 128), 1)
    row = lax.broadcasted_iota(jnp.int32, (24, 1), 0)
    risk = jnp.zeros((24, 1), f32)
    loading = jnp.zeros((24, 1), f32)
    for b in range(BUCKETS):
        risk = jnp.where(row == b, weight[b], risk)
        loading = jnp.where(row == b, load[b], loading)
    real = row < BUCKETS
    tenor_part = jnp.where(lane < TENORS, gather, 0.0)
    sums = jnp.sum(tenor_part, 1, keepdims=True)
    tenor_square = jnp.sum(tenor_part * tenor_part, 1, keepdims=True)
    own_square = gather[:, TENORS : TENORS + 1]
    name_square = gather[:, TENORS + 1 : TENORS + 2]
    columns = []
    row8 = lax.broadcasted_iota(jnp.int32, (8, 128), 0)
    capitals = jnp.zeros((8, 128), f32)
    for s in range(SCEN):
        level = [float(v) for v in LEVELS[s]]
        form = level[3] * sums * sums + (level[2] - level[3]) * tenor_square
        form = form + (level[1] - level[3]) * name_square + float(SAME_BOTH[s]) * own_square
        root = jnp.sqrt(form + 1e-6)
        radius = jnp.sqrt(root * root + sums * sums)
        capped = sums * root / radius
        pulled = jnp.where(real, loading * capped, 0.0)
        loaded = jnp.sum(pulled, 0, keepdims=True)
        squares = jnp.sum(pulled * pulled, 0, keepdims=True)
        cross = CROSS * SCENARIO[s]
        inside = jnp.sum(jnp.where(real, root * root, 0.0), 0, keepdims=True)
        cap = jnp.sqrt(inside + cross * (loaded * loaded - squares))
        cross_pull = cross * (loading * loaded - loading * loading * capped) / cap
        ratio = sums / radius
        share = root / radius
        coef_form = (root / cap + cross_pull * ratio * ratio * ratio) / root
        coef_sum = cross_pull * share * share * share
        scale = risk / cap
        columns.append(
            [
                (scale * coef_form * SCENARIO[s])[:BUCKETS],
                (scale * coef_form * (1.0 - SCENARIO[s]))[:BUCKETS],
                (scale * coef_sum)[:BUCKETS],
            ]
        )
        capitals = jnp.where(row8 == s, cap, capitals)
    capital[...] = capitals
    column = []
    for s in range(SCEN):
        column.append(jnp.concatenate(columns[s] + [jnp.zeros((2, 1), f32)], 0))
        mix[s] = jnp.broadcast_to(column[s][:ROWS] * float(NODES), (ROWS, 128))
    for p in range(parts):
        block = place[p]
        rows = pl.ds(pl.multiple_of(block * length, 128), length)
        value = alloc[:, rows]
        out = jnp.concatenate(
            [jnp.sum(value * (column[s] * float(trades_total)), 0, keepdims=True) for s in range(SCEN)],
            0,
        )
        if p < parts // 2:
            keep[p] = out
        else:
            send[p - parts // 2] = out


def bit_reverse(value, bits):
    return sum(((value >> i) & 1) << (bits - 1 - i) for i in range(bits))


def local(
    sensitivity,
    block_count,
    trade_node,
    factor_bucket,
    risk_weight,
    bucket_loading,
    *,
    trade_size,
    factor_size,
):
    trade_rows, width = sensitivity.shape
    trades_total = trade_rows * trade_size
    devices = trade_size * factor_size
    trade_bits = trade_size.bit_length() - 1
    factor_bits = factor_size.bit_length() - 1
    bits = trade_bits + factor_bits
    inner = (NODES // devices).bit_length() - 1
    t = lax.axis_index("trade")
    f = lax.axis_index("factor")
    me = t * factor_size + f

    def exchange(x, bit_of):
        pairs = [(o, o ^ (1 << bit_of(o))) for o in range(devices)]
        return lax.ppermute(x, AXES, pairs)

    upper_f = list(range(1, factor_bits))
    all_t = list(range(factor_bits, bits))
    orders = [upper_f + all_t, all_t[:2] + upper_f + all_t[2:]]
    places = [7, 11, 10, 9, 8, 6, 5, 4, 3, 2, 1, 0]
    spots = [[0] * bits, [0] * bits]
    for c in range(2):
        for i, bit in enumerate([0] + orders[c]):
            spots[c][bit] = 1 << places[i]
    block_order = jnp.array(
        [bit_reverse(p, factor_bits) for p in range(factor_size)], jnp.int32
    ) ^ f.astype(jnp.int32)
    bucket = lax.dynamic_slice_in_dim(factor_bucket, f * width, width, 0)[None, :]
    tenor = (jnp.arange(width, dtype=jnp.int32) % TENORS)[None, :]

    by_factor = pltpu.with_memory_space_constraint(sensitivity.T, pltpu.HBM)
    held, raw = call(
        totals_kernel,
        (pltpu.VMEM((width, trade_rows), bf16), shape(1, width)),
        [SMEM, ANY],
        (VMEM, VMEM),
        "totals",
        scratch=[pltpu.VMEM((width, 128), f32), pltpu.SemaphoreType.DMA((width // PIECE,))],
        flops=10**7,
    )(block_count, by_factor)

    low_hot, high_hot, spread_hot, tenor_hot, factor_weight = call(
        functools.partial(tables_kernel, spots=spots),
        (
            pltpu.VMEM((LOW, trade_rows), bf16),
            pltpu.VMEM((HIGH, trade_rows), bf16),
            pltpu.VMEM((56, width), f32),
            pltpu.VMEM((24 * TENORS, width), f32),
            pltpu.VMEM((1, width), f32),
        ),
        [SMEM, SMEM, VMEM, VMEM, VMEM],
        (VMEM,) * 5,
        "tables",
        flops=10**7,
    )(me.astype(jnp.int32)[None], risk_weight, trade_node[None, :], bucket, tenor)

    other = None
    for i in range(trade_bits):
        if other is not None:
            raw = raw + other
        other = exchange(raw, lambda o, i=i: factor_bits + i)

    spread, sums = call(
        weights_kernel,
        (pltpu.VMEM((128, width), bf16), shape(24, 128)),
        [VMEM] * 6,
        (VMEM, VMEM),
        "weights",
        flops=10**6,
    )(raw, other, factor_weight, tenor, spread_hot, tenor_hot)

    tenors = call(
        ones_kernel,
        pltpu.VMEM((24 * TENORS, trade_rows), f32),
        [VMEM, VMEM],
        VMEM,
        "ones",
        flops=2 * 128 * width * trade_rows,
    )(tenor_hot, held)

    near = call(
        spread_kernel,
        pltpu.VMEM((56, trade_rows), f32),
        [VMEM, VMEM],
        VMEM,
        "spread",
        flops=2 * 128 * width * trade_rows,
    )(spread, held)

    more = None
    for i in range(factor_bits):
        if more is not None:
            sums = sums + more
        more = exchange(sums, lambda o, i=i: i)

    alloc, total, keep, send = call(
        nodes_kernel,
        (
            pltpu.VMEM((56, trade_rows), f32),
            shape(24, 128),
            shape(HIGH, ROWS, LOW // 2),
            shape(HIGH, ROWS, LOW // 2),
        ),
        [SMEM, VMEM, VMEM, VMEM, VMEM, VMEM, VMEM],
        (VMEM,) * 4,
        "nodes",
        scratch=[pltpu.VMEM((64, trade_rows), bf16)],
        flops=2 * 1024 * trade_rows * LOW,
    )(block_count, sums, more, near, tenors, low_hot, high_hot)

    length = trade_rows // factor_size
    trade_keep, trade_send, mix, capital = call(
        functools.partial(capital_kernel, trades_total=trades_total),
        (
            shape(factor_size // 2, SCEN, length),
            shape(factor_size // 2, SCEN, length),
            shape(SCEN, ROWS, 128),
            shape(8, 128),
        ),
        [SMEM, SMEM, SMEM, VMEM, VMEM],
        (VMEM,) * 4,
        "capital",
        flops=10**7,
    )(block_order, risk_weight, bucket_loading, total, alloc)

    keep = keep + exchange(send, lambda o: 0)
    for i in range(bits - 1):
        if keep.shape[0] > 1:
            half = keep.shape[0] // 2
            send, keep = keep[half:], keep[:half]
        else:
            half = keep.shape[2] // 2
            send, keep = keep[..., half:], keep[..., :half]
        keep = keep + exchange(send, lambda o, i=i: orders[o & 1][i])
    keep = keep[0]

    trade_keep = trade_keep + exchange(trade_send, lambda o: 0)
    for i in range(1, factor_bits):
        half = trade_keep.shape[0] // 2
        trade_send, trade_keep = trade_keep[half:], trade_keep[:half]
        trade_keep = trade_keep + exchange(trade_send, lambda o, i=i: i)

    mixed = mix[:, :, : keep.shape[1]] * keep[None]
    node_alloc = mixed.reshape(SCEN, 3, BUCKETS, keep.shape[1]).sum(1)
    capital_scaled = capital[:SCEN, 0] / trades_total**0.5
    return (capital_scaled, trade_keep[0], node_alloc)


def solution(mesh):
    sizes = dict(mesh.shape)
    return jax.shard_map(
        functools.partial(local, trade_size=sizes["trade"], factor_size=sizes["factor"]),
        mesh=mesh,
        in_specs=(P("trade", "factor"), P("trade"), P("trade"), P(), P(), P()),
        out_specs=(P(), P(None, ("trade", "factor")), P(None, None, ("trade", "factor"))),
        check_vma=False,
    )
```

```python
import functools

import jax
import jax.numpy as jnp
import numpy as np
from jax import lax
from jax.experimental import pallas as pl
from jax.experimental.pallas import tpu as pltpu
from jax.sharding import PartitionSpec as P

TENORS = 5
BUCKETS = 18
GROUP = 24
SCEN = 3
NODES = 4096
BLOCK = 512
LANES = 128
PIECE = 256
LOW = 256
HIGH = NODES // LOW
AXES = ("trade", "factor")
MIB = 1 << 20

BASE = np.array([1.0, 0.65, 0.35, 0.2275], np.float32)
LEVELS = np.stack([BASE, np.minimum(1.25 * BASE, 1.0), np.maximum(2.0 * BASE - 1.0, 0.75 * BASE)])
SCENARIO = (1.0, 1.25, 0.75)
CROSS = 0.5
SAME_BOTH = LEVELS[:, 0] - LEVELS[:, 1] - LEVELS[:, 2] + LEVELS[:, 3]

SMEM = pl.BlockSpec(memory_space=pltpu.SMEM)
VMEM = pl.BlockSpec(memory_space=pltpu.VMEM)
ANY = pl.BlockSpec(memory_space=pl.ANY)
f32 = jnp.float32
bf16 = jnp.bfloat16


def shape(*dims, dtype=f32):
    return jax.ShapeDtypeStruct(dims, dtype)


def call(kernel, out_shape, in_specs, out_specs, name, scratch=(), flops=0, alias=None, limit=8):
    return pl.pallas_call(
        kernel,
        out_shape=out_shape,
        in_specs=in_specs,
        out_specs=out_specs,
        scratch_shapes=list(scratch),
        name=name,
        input_output_aliases=alias or {},
        compiler_params=pltpu.CompilerParams(vmem_limit_bytes=limit * MIB),
        cost_estimate=pl.CostEstimate(flops=flops, bytes_accessed=1 << 16, transcendentals=0),
    )


def dot(a, b):
    return lax.dot_general(a, b, (((1,), (0,)), ((), ())), preferred_element_type=f32)


def dot_t(a, b):
    return lax.dot_general(a, b, (((1,), (1,)), ((), ())), preferred_element_type=f32)


def totals_kernel(count_hbm, sens, held, raw, count, sems, count_sem):
    width, trades = sens.shape
    pieces = [(start, min(PIECE, width - start)) for start in range(0, width, PIECE)]
    counting = pltpu.make_async_copy(count_hbm, count, count_sem)
    counting.start()
    copies = []
    for i, (start, rows) in enumerate(pieces):
        part = pl.ds(start, rows)
        copies.append(pltpu.make_async_copy(sens.at[part], held.at[part], sems.at[i]))
        copies[-1].start()
    counting.wait()
    ones = jnp.ones((16, 3 * LANES), bf16)

    def run(tiles):
        for copy, (start, rows) in zip(copies, pieces):
            copy.wait()
            chains = 1 if rows > 128 else 4
            totals = [None] * chains
            for i, (lane, live) in enumerate(tiles(rows)):
                part = held[start : start + rows, lane : lane + LANES].astype(f32)
                if live is not None:
                    part = jnp.where(live, part, 0.0)
                j = i % chains
                totals[j] = part if totals[j] is None else totals[j] + part
            value = sum(totals[1:], totals[0])
            upper = value.astype(bf16)
            value = value - upper.astype(f32)
            middle = value.astype(bf16)
            lower = (value - middle.astype(f32)).astype(bf16)
            parts = jnp.concatenate([upper, middle, lower], 1)
            raw[:, start : start + rows] = dot_t(ones, parts)[:1]

    full = count[0] == BLOCK

    @pl.when(full)
    def _():
        run(lambda rows: [(lane, None) for lane in range(0, trades, LANES)])

    @pl.when(jnp.logical_not(full))
    def _():
        def tiles(rows):
            slot = lax.broadcasted_iota(jnp.int32, (rows, LANES), 1)
            return [(i * BLOCK, slot < count[i]) for i in range(trades // BLOCK)]

        run(tiles)


def tables_kernel(
    count,
    weight,
    own,
    nodes,
    buckets,
    low_hot,
    pair_hot,
    tenor_hot,
    factor_weight,
    tenor,
    passed,
    mine,
    *,
    spots,
    factor_size,
):
    passed[...] = own[...]
    f = lax.axis_index("factor")
    me = lax.axis_index("trade") * factor_size + f
    bits = len(spots)
    inner = (NODES >> bits).bit_length() - 1
    node = nodes[...]
    other = (node >> inner) ^ me
    label = node & ((1 << inner) - 1)
    for i in range(bits):
        label = label + ((other >> i) & 1) * spots[i]
    low = label & (LOW - 1)
    high = label >> (LOW.bit_length() - 1)
    trades = node.shape[1]
    for start in range(0, trades, 512):
        part = pl.ds(start, 512)
        here = lax.broadcasted_iota(jnp.int32, (LOW, 512), 0) == low[:, start : start + 512]
        low_hot[:, part] = jnp.where(here, 1.0, 0.0).astype(bf16)
        row = lax.broadcasted_iota(jnp.int32, (2 * GROUP, 512), 0)
        away = high[:, start : start + 512] - jnp.where(row < GROUP, 0, 1)
        slot = lax.broadcasted_iota(jnp.int32, (2 * GROUP, 512), 1)
        away = jnp.where(slot < count[start // BLOCK], away, -1)
        for p in range(HIGH // 2):
            pair_hot[p, :, part] = jnp.where(away == 2 * p, 1.0, 0.0).astype(bf16)
    width = own.shape[1]
    for i in range(factor_size):

        @pl.when(f == i)
        def _(i=i):
            mine[...] = buckets[:, i * width : (i + 1) * width]

    bucket = mine[...]
    place = lax.broadcasted_iota(jnp.int32, (1, width), 1)
    column = lax.rem(place, TENORS)
    tenor[...] = column
    row = lax.broadcasted_iota(jnp.int32, (GROUP, width), 0)
    for m in range(TENORS):
        hot = (row == bucket) & (column == m)
        tenor_hot[GROUP * m : GROUP * (m + 1), :] = jnp.where(hot, 1.0, 0.0)
    total = jnp.zeros((1, width), f32)
    for b in range(BUCKETS):
        total = jnp.where(bucket == b, weight[b], total)
    factor_weight[...] = total


def multiply(weights, held, product):
    for start in range(0, held.shape[1], BLOCK):
        part = pl.ds(start, BLOCK)
        product[:, part] = dot(weights, held[:, part])


def twice(value):
    return jnp.concatenate([value, value], 0).astype(bf16)


def ones_kernel(own, tenor_hot, held, product, rounded, passed):
    passed[...] = own[...]
    hot = tenor_hot[...]
    every = sum(hot[GROUP * m : GROUP * (m + 1)] for m in range(TENORS))
    fill = jnp.zeros((8, held.shape[0]), f32)
    hot = jnp.concatenate([hot[: GROUP * (TENORS - 1)], every, fill], 0).astype(bf16)
    multiply(hot, held, product)
    rounded[...] = twice(product[GROUP * (TENORS - 1) : GROUP * TENORS])


def sums_by_node(rounded, low_hot, pair_hot, first, keep, send):
    value = rounded[...]
    masked = jnp.concatenate([value * pair_hot[p] for p in range(HIGH // 2)], 0)
    out = dot_t(masked, low_hot[...])
    for h in range(HIGH):
        rows = out[GROUP * h : GROUP * h + BUCKETS]
        keep[h, first : first + BUCKETS] = rows[:, : LOW // 2]
        send[h, first : first + BUCKETS] = rows[:, LOW // 2 :]


def ones_nodes_kernel(own, rounded, low_hot, pair_hot, keep, send, passed):
    passed[...] = own[...]
    sums_by_node(rounded, low_hot, pair_hot, BUCKETS, keep, send)


def weights_kernel(*refs):
    *raws, factor_weight, tenor, tenor_hot, spread, sums = refs
    width = tenor.shape[1]
    weighted = factor_weight[...] * sum(r[...] for r in raws)
    own_tenor = tenor[...]
    name = weighted
    for d in range(1, TENORS):
        zeros = jnp.zeros((1, d), f32)
        after = jnp.concatenate([weighted[:, d:], zeros], 1)
        before = jnp.concatenate([zeros, weighted[:, : width - d]], 1)
        name = name + jnp.where(own_tenor < TENORS - d, after, 0.0)
        name = name + jnp.where(own_tenor >= d, before, 0.0)
    near = float(LEVELS[0, 1] - LEVELS[0, 3]) * name + float(SAME_BOTH[0]) * weighted
    hot = tenor_hot[:GROUP, :]
    for m in range(1, TENORS):
        hot = hot + tenor_hot[GROUP * m : GROUP * (m + 1), :]
    full = jnp.concatenate([hot * weighted, hot * near], 0)
    upper = full.astype(bf16).astype(f32)
    fill = jnp.zeros((32, width), f32)
    spread[...] = jnp.concatenate([upper, full - upper, fill], 0).astype(bf16)
    lane = lax.broadcasted_iota(jnp.int32, (GROUP, LANES), 1)
    out = jnp.zeros((GROUP, LANES), f32)
    square = jnp.zeros((GROUP, 1), f32)
    for m in range(TENORS):
        hot = tenor_hot[GROUP * m : GROUP * (m + 1), :]
        part = hot * weighted
        out = jnp.where(lane == m, jnp.sum(part, 1, keepdims=True), out)
        square = square + jnp.sum(part * weighted, 1, keepdims=True)
        if m == 0:
            names = jnp.sum(hot * (name * name), 1, keepdims=True)
    out = jnp.where(lane == TENORS, square, out)
    out = jnp.where(lane == TENORS + 1, names, out)
    sums[...] = out


def spread_kernel(spread, held, product, rounded):
    multiply(spread[...], held, product)
    rounded[...] = twice(product[:GROUP] + product[2 * GROUP : 3 * GROUP])


def weighted_nodes_kernel(rounded, low_hot, pair_hot, _, __, keep, send):
    sums_by_node(rounded, low_hot, pair_hot, 0, keep, send)


def product_nodes_kernel(*refs):
    *sums, near, tenors, low_hot, pair_hot, _, _, alloc, total, keep, send, rounded = refs
    gather = sum(r[...] for r in sums)
    total[...] = gather
    lane = lax.broadcasted_iota(jnp.int32, (GROUP, LANES), 1)
    bucket = jnp.sum(jnp.where(lane < TENORS, gather, 0.0), 1, keepdims=True)
    same = float(LEVELS[0, 2] - LEVELS[0, 3])
    last = gather[:, TENORS - 1 : TENORS]
    pull = [same * (gather[:, m : m + 1] - last) for m in range(TENORS - 1)]
    pull.append(same * last + float(LEVELS[0, 3]) * bucket)
    for start in range(0, near.shape[1], BLOCK):
        part = pl.ds(start, BLOCK)
        value = near[GROUP : 2 * GROUP, part] + near[3 * GROUP : 4 * GROUP, part]
        for m in range(TENORS):
            value = value + pull[m] * tenors[GROUP * m : GROUP * (m + 1), part]
        alloc[:, part] = value
        rounded[:, part] = twice(value)
    sums_by_node(rounded, low_hot, pair_hot, 2 * BUCKETS, keep, send)


def join_kernel(own, keep, more, passed, *chunks):
    passed[...] = own[...]
    size = chunks[0].shape[0]
    for c, chunk in enumerate(chunks):
        part = pl.ds(c * size, size)
        chunk[...] = keep[part] + more[part]


def capital_kernel(
    count, weight, load, total, product, near, tenors, keep, send, mix, capital, *, trades_total, parts
):
    half = keep.shape[0]
    length = product.shape[1] // parts
    gather = total[...]
    lane = lax.broadcasted_iota(jnp.int32, (GROUP, LANES), 1)
    row = lax.broadcasted_iota(jnp.int32, (GROUP, 1), 0)
    real = row < BUCKETS
    risk = jnp.zeros((GROUP, 1), f32)
    loading = jnp.zeros((GROUP, 1), f32)
    for b in range(BUCKETS):
        risk = jnp.where(row == b, weight[b], risk)
        loading = jnp.where(row == b, load[b], loading)
    tenor_part = jnp.where(lane < TENORS, gather, 0.0)
    sums = jnp.sum(tenor_part, 1, keepdims=True)
    tenor_square = jnp.sum(tenor_part * tenor_part, 1, keepdims=True)
    own_square = gather[:, TENORS : TENORS + 1]
    name_square = gather[:, TENORS + 1 : TENORS + 2]
    columns = []
    row8 = lax.broadcasted_iota(jnp.int32, (8, LANES), 0)
    capitals = jnp.zeros((8, LANES), f32)
    for s in range(SCEN):
        level = [float(v) for v in LEVELS[s]]
        form = level[3] * sums * sums + (level[2] - level[3]) * tenor_square
        form = form + (level[1] - level[3]) * name_square + float(SAME_BOTH[s]) * own_square
        root = jnp.sqrt(form + 1e-6)
        radius = jnp.sqrt(root * root + sums * sums)
        capped = sums * root / radius
        pulled = jnp.where(real, loading * capped, 0.0)
        loaded = jnp.sum(pulled, 0, keepdims=True)
        squares = jnp.sum(pulled * pulled, 0, keepdims=True)
        cross = CROSS * SCENARIO[s]
        inside = jnp.sum(jnp.where(real, root * root, 0.0), 0, keepdims=True)
        cap = jnp.sqrt(inside + cross * (loaded * loaded - squares))
        cross_pull = cross * (loading * loaded - loading * loading * capped) / cap
        ratio = sums / radius
        share = root / radius
        coef_form = (root / cap + cross_pull * ratio * ratio * ratio) / root
        coef_sum = cross_pull * share * share * share
        scale = jnp.where(real, risk / cap, 0.0)
        columns.append(
            [
                scale * coef_form * (1.0 - SCENARIO[s]),
                scale * coef_sum,
                scale * coef_form * SCENARIO[s],
            ]
        )
        capitals = jnp.where(row8 == s, cap, capitals)
    capital[...] = capitals
    for s in range(SCEN):
        column = jnp.concatenate([c[:BUCKETS] for c in columns[s]], 0)
        mix[s] = jnp.broadcast_to(column * float(NODES), (3 * BUCKETS, LANES))
    f = lax.axis_index("factor")
    bits = parts.bit_length() - 1
    for p in range(parts):
        block = f ^ sum(((p >> i) & 1) << (bits - 1 - i) for i in range(bits))
        rows = pl.ds(pl.multiple_of(block * length, LANES), length)
        values = [
            near[:GROUP, rows] + near[2 * GROUP : 3 * GROUP, rows],
            tenors[GROUP * (TENORS - 1) : GROUP * TENORS, rows],
            product[:, rows],
        ]
        slot = lax.broadcasted_iota(jnp.int32, (1, BLOCK), 1)
        live = [
            jnp.where(slot < count[block * (length // BLOCK) + i], 1.0, 0.0)
            for i in range(length // BLOCK)
        ]
        live = jnp.concatenate(live, 1)
        for s in range(SCEN):
            out = sum(v * (c * float(trades_total)) for v, c in zip(values, columns[s]))
            out = jnp.sum(out, 0, keepdims=True) * live
            for j in range(length // LANES):
                place = s * (length // LANES) + j
                piece = out[:, j * LANES : (j + 1) * LANES]
                if p < half:
                    keep[p, place : place + 1] = piece
                else:
                    send[p - half, place : place + 1] = piece


def finish_kernel(mix, capital, trade_keep, trade_more, *refs, scale):
    *pieces, scaled, trades, nodes = refs
    total = sum(p[...] for p in pieces)
    for s in range(SCEN):
        mixed = mix[s][:, : total.shape[1]] * total
        nodes[s] = sum(mixed[BUCKETS * j : BUCKETS * (j + 1)] for j in range(3))
    value = trade_keep[...] + trade_more[...]
    count = value.shape[0] // SCEN
    for s in range(SCEN):
        for j in range(count):
            place = s * count + j
            trades[s : s + 1, j * LANES : (j + 1) * LANES] = value[place : place + 1]
    for s in range(SCEN):
        scaled[s] = jnp.max(capital[s : s + 1, :]) * scale


def local(
    sensitivity,
    block_count,
    trade_node,
    factor_bucket,
    risk_weight,
    bucket_loading,
    *,
    trade_size,
    factor_size,
):
    trade_rows, width = sensitivity.shape
    trades_total = trade_rows * trade_size
    devices = trade_size * factor_size
    trade_bits = trade_size.bit_length() - 1
    factor_bits = factor_size.bit_length() - 1
    bits = trade_bits + factor_bits

    def exchange(x, mask):
        return lax.ppermute(x, AXES, [(o, o ^ mask) for o in range(devices)])

    over_factor = list(range(1, factor_bits))
    over_trade = list(range(factor_bits, bits))
    groups = [over_trade[:2], over_factor[:1] + over_trade[2:3]]
    groups += [[b] for b in over_factor[1:] + over_trade[3:]]
    order = [0] + sum(groups, [])
    places = [7, 11, 10, 9, 8, 6, 5, 4, 3, 2, 1, 0]
    spots = [0] * bits
    for i, bit in enumerate(order):
        spots[bit] = 1 << places[i]

    by_factor = pltpu.with_memory_space_constraint(sensitivity.T, pltpu.HBM)
    held, raw = call(
        totals_kernel,
        (pltpu.VMEM((width, trade_rows), bf16), shape(1, width)),
        [ANY, ANY],
        (VMEM, VMEM),
        "totals",
        scratch=[
            pltpu.SMEM(block_count.shape, jnp.int32),
            pltpu.SemaphoreType.DMA((-(-width // PIECE),)),
            pltpu.SemaphoreType.DMA,
        ],
        flops=10**7,
    )(pltpu.with_memory_space_constraint(block_count, pltpu.HBM), by_factor)

    rows = pltpu.VMEM((GROUP, trade_rows), f32)
    multiplied = pltpu.VMEM((128, trade_rows), f32)
    rounded = pltpu.VMEM((2 * GROUP, trade_rows), bf16)
    trade_mask = [1 << b for b in over_trade]
    other = exchange(raw, trade_mask[0])
    low_hot, pair_hot, tenor_hot, factor_weight, tenor, raw = call(
        functools.partial(tables_kernel, spots=spots, factor_size=factor_size),
        (
            pltpu.VMEM((LOW, trade_rows), bf16),
            pltpu.VMEM((HIGH // 2, 2 * GROUP, trade_rows), bf16),
            pltpu.VMEM((GROUP * TENORS, width), f32),
            pltpu.VMEM((1, width), f32),
            pltpu.VMEM((1, width), jnp.int32),
            shape(1, width),
        ),
        [SMEM, SMEM, VMEM, VMEM, VMEM],
        (VMEM,) * 6,
        "tables",
        scratch=[pltpu.VMEM((1, width), jnp.int32)],
        flops=10**7,
    )(block_count, risk_weight, raw, trade_node[None, :], factor_bucket[None, :])

    for mask in trade_mask[3:]:
        raw = raw + other
        other = exchange(raw, mask)
    raw = raw + other
    others = [exchange(raw, mask) for mask in (trade_mask[1] + trade_mask[2], trade_mask[2], trade_mask[1])]
    tenors, ones_rounded, raw = call(
        ones_kernel,
        (multiplied, rounded, shape(1, width)),
        [VMEM] * 3,
        (VMEM,) * 3,
        "ones",
        flops=2 * 128 * width * trade_rows,
    )(raw, tenor_hot, held)

    all_nodes = (HIGH, 3 * BUCKETS, LOW // 2)
    nodes_flops = 2 * 512 * trade_rows * LOW
    keep, send, raw = call(
        ones_nodes_kernel,
        (pltpu.VMEM(all_nodes, f32), pltpu.VMEM(all_nodes, f32), shape(1, width)),
        [VMEM] * 4,
        (VMEM,) * 3,
        "ones_nodes",
        flops=nodes_flops,
    )(raw, ones_rounded, low_hot, pair_hot)

    spread, sums = call(
        weights_kernel,
        (pltpu.VMEM((128, width), bf16), shape(GROUP, LANES)),
        [VMEM] * (4 + len(others)),
        (VMEM, VMEM),
        "weights",
        flops=10**6,
    )(raw, *others, factor_weight, tenor, tenor_hot)

    others = [exchange(sums, mask) for mask in range(1, factor_size)]
    near, weighted_rounded = call(
        spread_kernel,
        (multiplied, rounded),
        [VMEM] * 2,
        (VMEM,) * 2,
        "spread",
        flops=2 * 128 * width * trade_rows,
    )(spread, held)
    keep, send = call(
        weighted_nodes_kernel,
        (pltpu.VMEM(all_nodes, f32),) * 2,
        [VMEM] * 5,
        (VMEM,) * 2,
        "weighted_nodes",
        alias={3: 0, 4: 1},
        flops=nodes_flops,
    )(weighted_rounded, low_hot, pair_hot, keep, send)

    product, total, keep, send = call(
        product_nodes_kernel,
        (rows, shape(GROUP, LANES), pltpu.VMEM(all_nodes, f32), pltpu.VMEM(all_nodes, f32)),
        [VMEM] * (7 + len(others)),
        (VMEM,) * 4,
        "product_nodes",
        alias={5 + len(others): 2, 6 + len(others): 3},
        scratch=[rounded],
        flops=nodes_flops,
    )(sums, *others, near, tenors, low_hot, pair_hot, keep, send)
    from_core = exchange(send, 1)

    trade_shape = shape(factor_size // 2, SCEN * trade_rows // factor_size // LANES, LANES)
    trade_keep, trade_send, mix, capital = call(
        functools.partial(capital_kernel, trades_total=trades_total, parts=factor_size),
        (trade_shape, trade_shape, shape(SCEN, 3 * BUCKETS, LANES), shape(8, LANES)),
        [SMEM, SMEM, SMEM] + [VMEM] * 4,
        (VMEM,) * 4,
        "capital",
        flops=10**7,
    )(block_count, risk_weight, bucket_loading, total, product, near, tenors)

    count = 1 << len(groups[0])
    trade_send, *chunks = call(
        join_kernel,
        (trade_shape,) + (shape(HIGH // count, 3 * BUCKETS, LOW // 2),) * count,
        [VMEM] * 3,
        (VMEM,) * (1 + count),
        "join",
        flops=10**6,
    )(trade_send, keep, from_core)
    trade_more = exchange(trade_send, 1)
    for i, group in enumerate(groups):
        count = 1 << len(group)
        if i > 0:
            axis = 0 if keep.shape[0] > 1 else 2
            chunks = jnp.split(keep, count, axis)
        pieces = [chunks[0]]
        for c in range(count - 1, 0, -1):
            part = [b for j, b in enumerate(group) if (c >> (len(group) - 1 - j)) & 1]
            mask = sum(1 << b for b in part)
            message = chunks[c]
            if len(part) == 1 and part[0] in over_factor:
                trade_send, trade_keep = jnp.split(trade_keep + trade_more, 2, 0)[::-1]
                if message.shape[2] == LANES:
                    cut = trade_send.shape[0] * trade_send.shape[1]
                    message = jnp.concatenate(
                        [trade_send.reshape(cut, LANES), message.reshape(-1, LANES)], 0
                    )
                    message = exchange(message, mask)
                    trade_more = message[:cut].reshape(trade_send.shape)
                    message = message[cut:].reshape(chunks[c].shape)
                else:
                    trade_more = exchange(trade_send, mask)
                    message = exchange(message, mask)
            else:
                message = exchange(message, mask)
            pieces.append(message)
        if i + 1 < len(groups):
            keep = sum(pieces[1:], pieces[0])
    return call(
        functools.partial(finish_kernel, scale=1.0 / trades_total**0.5),
        (
            shape(SCEN),
            shape(SCEN, trade_rows // factor_size),
            shape(SCEN, BUCKETS, NODES // devices),
        ),
        [VMEM] * (4 + len(pieces)),
        (SMEM, VMEM, VMEM),
        "finish",
        flops=10**6,
    )(mix, capital, trade_keep[0], trade_more[0], *[p[0] for p in pieces])


def solution(mesh):
    sizes = dict(mesh.shape)
    return jax.shard_map(
        functools.partial(local, trade_size=sizes["trade"], factor_size=sizes["factor"]),
        mesh=mesh,
        in_specs=(P("trade", "factor"), P("trade"), P("trade"), P(), P(), P()),
        out_specs=(P(), P(None, ("trade", "factor")), P(None, None, ("trade", "factor"))),
        check_vma=False,
    )
```

```python
import functools

import jax
import jax.numpy as jnp
import numpy as np
from jax import lax
from jax.experimental import pallas as pl
from jax.experimental.pallas import tpu as pltpu
from jax.sharding import PartitionSpec as P

TENORS = 5
BUCKETS = 18
GROUP = 24
SCEN = 3
NODES = 4096
BLOCK = 512
LANES = 128
PIECE = 256
LOW = 256
HIGH = NODES // LOW
AXES = ("trade", "factor")
MIB = 1 << 20

BASE = np.array([1.0, 0.65, 0.35, 0.2275], np.float32)
LEVELS = np.stack([BASE, np.minimum(1.25 * BASE, 1.0), np.maximum(2.0 * BASE - 1.0, 0.75 * BASE)])
SCENARIO = (1.0, 1.25, 0.75)
CROSS = 0.5
SAME_BOTH = LEVELS[:, 0] - LEVELS[:, 1] - LEVELS[:, 2] + LEVELS[:, 3]

SMEM = pl.BlockSpec(memory_space=pltpu.SMEM)
VMEM = pl.BlockSpec(memory_space=pltpu.VMEM)
ANY = pl.BlockSpec(memory_space=pl.ANY)
f32 = jnp.float32
bf16 = jnp.bfloat16


def shape(*dims, dtype=f32):
    return jax.ShapeDtypeStruct(dims, dtype)


def call(kernel, out_shape, in_specs, out_specs, name, scratch=(), flops=0, alias=None, limit=8):
    return pl.pallas_call(
        kernel,
        out_shape=out_shape,
        in_specs=in_specs,
        out_specs=out_specs,
        scratch_shapes=list(scratch),
        name=name,
        input_output_aliases=alias or {},
        compiler_params=pltpu.CompilerParams(vmem_limit_bytes=limit * MIB),
        cost_estimate=pl.CostEstimate(flops=flops, bytes_accessed=1 << 16, transcendentals=0),
    )


def dot(a, b):
    return lax.dot_general(a, b, (((1,), (0,)), ((), ())), preferred_element_type=f32)


def dot_t(a, b):
    return lax.dot_general(a, b, (((1,), (1,)), ((), ())), preferred_element_type=f32)


def three_parts(value):
    upper = value.astype(bf16).astype(f32)
    middle = (value - upper).astype(bf16).astype(f32)
    return upper, middle, value - upper - middle


def fill_tables(
    count, weight, nodes, bucket, low_hot, pair_hot, hot, ones_hot, factor_weight, me, spots
):
    bits = len(spots)
    inner = (NODES >> bits).bit_length() - 1
    node = nodes[...]
    other = (node >> inner) ^ me
    label = node & ((1 << inner) - 1)
    for i in range(bits):
        label = label + ((other >> i) & 1) * spots[i]
    low = label & (LOW - 1)
    high = label >> (LOW.bit_length() - 1)
    for i in range(node.shape[1] // BLOCK):
        part = slice(i * BLOCK, (i + 1) * BLOCK)
        here = lax.broadcasted_iota(jnp.int32, (LOW, BLOCK), 0) == low[:, part]
        low_hot[:, part] = jnp.where(here, 1.0, 0.0).astype(bf16)
        row = lax.broadcasted_iota(jnp.int32, (2 * GROUP, BLOCK), 0)
        away = high[:, part] - jnp.where(row < GROUP, 0, 1)
        slot = lax.broadcasted_iota(jnp.int32, (2 * GROUP, BLOCK), 1)
        away = jnp.where(slot < count[i], away, -1)
        for p in range(HIGH // 2):
            pair_hot[p, :, part] = jnp.where(away == 2 * p, 1.0, 0.0).astype(bf16)
    width = bucket.shape[1]
    column = lax.rem(lax.broadcasted_iota(jnp.int32, (1, width), 1), TENORS)
    row = lax.broadcasted_iota(jnp.int32, (GROUP, width), 0)
    every = row == bucket
    by_tenor = [jnp.where(every & (column == m), 1.0, 0.0) for m in range(TENORS)]
    fill = [jnp.zeros((8, width), f32)]
    hot[...] = jnp.concatenate(by_tenor + fill, 0).astype(bf16)
    every = [jnp.where(every, 1.0, 0.0)]
    ones_hot[...] = jnp.concatenate(by_tenor[:-1] + every + fill, 0).astype(bf16)
    total = jnp.zeros((1, width), f32)
    for b in range(BUCKETS):
        total = jnp.where(bucket == b, weight[b], total)
    factor_weight[...] = total


def totals_kernel(
    count_hbm,
    weight_hbm,
    nodes_hbm,
    buckets_hbm,
    sens,
    held,
    raw,
    low_hot,
    pair_hot,
    hot,
    ones_hot,
    factor_weight,
    count,
    weight,
    nodes,
    buckets,
    bucket,
    sems,
    small_sems,
    *,
    spots,
    factor_size,
):
    width, trades = sens.shape
    pieces = [(start, min(PIECE, width - start)) for start in range(0, width, PIECE)]
    small = []
    for i, (source, target) in enumerate(
        [(count_hbm, count), (weight_hbm, weight), (nodes_hbm, nodes), (buckets_hbm, buckets)]
    ):
        small.append(pltpu.make_async_copy(source, target, small_sems.at[i]))
        small[-1].start()
    copies = []
    for i, (start, rows) in enumerate(pieces):
        part = pl.ds(start, rows)
        copies.append(pltpu.make_async_copy(sens.at[part], held.at[part], sems.at[i]))
    copies[0].start()
    for copy in small:
        copy.wait()
    for copy in copies[1:]:
        copy.start()
    f = lax.axis_index("factor")
    me = lax.axis_index("trade") * factor_size + f
    for i in range(factor_size):

        @pl.when(f == i)
        def _(i=i):
            first, off = divmod(i * width, LANES)
            last = -(-(off + width) // LANES) + first
            row = jnp.concatenate([buckets[r : r + 1] for r in range(first, last)], 1)
            bucket[...] = row[:, off : off + width]

    fill_tables(
        count,
        weight,
        nodes,
        bucket[...],
        low_hot,
        pair_hot,
        hot,
        ones_hot,
        factor_weight,
        me,
        spots,
    )
    ones = jnp.ones((16, 3 * LANES), bf16)

    def run(tiles):
        for copy, (start, rows) in zip(copies, pieces):
            copy.wait()
            chains = 1 if rows > 128 else 4
            totals = [None] * chains
            for i, (lane, live) in enumerate(tiles(rows)):
                part = held[start : start + rows, lane : lane + LANES].astype(f32)
                if live is not None:
                    part = jnp.where(live, part, 0.0)
                j = i % chains
                totals[j] = part if totals[j] is None else totals[j] + part
            value = sum(totals[1:], totals[0])
            parts = jnp.concatenate(three_parts(value), 1).astype(bf16)
            raw[:, start : start + rows] = dot_t(ones, parts)[:1]

    full = count[0] == BLOCK

    @pl.when(full)
    def _():
        run(lambda rows: [(lane, None) for lane in range(0, trades, LANES)])

    @pl.when(jnp.logical_not(full))
    def _():
        def tiles(rows):
            slot = lax.broadcasted_iota(jnp.int32, (rows, LANES), 1)
            return [(i * BLOCK, slot < count[i]) for i in range(trades // BLOCK)]

        run(tiles)


def multiply(weights, held, product):
    for start in range(0, held.shape[1], BLOCK):
        part = pl.ds(start, BLOCK)
        product[:, part] = dot(weights, held[:, part])


def twice(value):
    return jnp.concatenate([value, value], 0).astype(bf16)


def ones_kernel(own, ones_hot, held, product, rounded, passed):
    passed[...] = own[...]
    multiply(ones_hot[...], held, product)
    rounded[...] = twice(product[GROUP * (TENORS - 1) : GROUP * TENORS])


def sums_by_node(rounded, low_hot, pair_hot, first, keep, send):
    value = rounded[...]
    masked = jnp.concatenate([value * pair_hot[p] for p in range(HIGH // 2)], 0)
    out = dot_t(masked, low_hot[...])
    for h in range(HIGH):
        rows = out[GROUP * h : GROUP * h + BUCKETS]
        keep[h, first : first + BUCKETS] = rows[:, : LOW // 2]
        send[h, first : first + BUCKETS] = rows[:, LOW // 2 :]


def ones_nodes_kernel(own, rounded, low_hot, pair_hot, keep, send, passed):
    passed[...] = own[...]
    sums_by_node(rounded, low_hot, pair_hot, BUCKETS, keep, send)


def weights_kernel(*refs):
    *raws, factor_weight, hot, ones_hot, spread, sums = refs
    width = factor_weight.shape[1]
    weighted = factor_weight[...] * sum(r[...] for r in raws)
    own_tenor = lax.rem(lax.broadcasted_iota(jnp.int32, (1, width), 1), TENORS)
    name = weighted
    for d in range(1, TENORS):
        zeros = jnp.zeros((1, d), f32)
        after = jnp.concatenate([weighted[:, d:], zeros], 1)
        before = jnp.concatenate([zeros, weighted[:, : width - d]], 1)
        name = name + jnp.where(own_tenor < TENORS - d, after, 0.0)
        name = name + jnp.where(own_tenor >= d, before, 0.0)
    near = float(LEVELS[0, 1] - LEVELS[0, 3]) * name + float(SAME_BOTH[0]) * weighted
    every = ones_hot[GROUP * (TENORS - 1) : GROUP * TENORS].astype(f32)
    full = jnp.concatenate([every * weighted, every * near], 0)
    upper = full.astype(bf16).astype(f32)
    fill = jnp.zeros((32, width), f32)
    spread[...] = jnp.concatenate([upper, full - upper, fill], 0).astype(bf16)
    lane = lax.broadcasted_iota(jnp.int32, (GROUP, LANES), 1)
    square = jnp.sum(every * (weighted * weighted), 1, keepdims=True)
    out = jnp.where(lane == TENORS, square, 0.0)
    first = jnp.where(own_tenor == 0, name, 0.0)
    names = jnp.sum(every * (first * first), 1, keepdims=True)
    out = jnp.where(lane == TENORS + 1, names, out)
    by_tenor = hot[...].astype(f32) * weighted
    for m in range(TENORS):
        part = jnp.sum(by_tenor[GROUP * m : GROUP * (m + 1)], 1, keepdims=True)
        out = jnp.where(lane == m, part, out)
    sums[...] = out


def spread_kernel(spread, held, product, rounded):
    multiply(spread[...], held, product)
    rounded[...] = twice(product[:GROUP] + product[2 * GROUP : 3 * GROUP])


def weighted_nodes_kernel(rounded, low_hot, pair_hot, _, __, keep, send):
    sums_by_node(rounded, low_hot, pair_hot, 0, keep, send)


def product_nodes_kernel(*refs):
    *sums, near, tenors, low_hot, pair_hot, _, _, alloc, total, keep, send, rounded = refs
    gather = sum(r[...] for r in sums)
    total[...] = gather
    lane = lax.broadcasted_iota(jnp.int32, (GROUP, LANES), 1)
    bucket = jnp.sum(jnp.where(lane < TENORS, gather, 0.0), 1, keepdims=True)
    same = float(LEVELS[0, 2] - LEVELS[0, 3])
    last = gather[:, TENORS - 1 : TENORS]
    pull = [same * (gather[:, m : m + 1] - last) for m in range(TENORS - 1)]
    pull.append(same * last + float(LEVELS[0, 3]) * bucket)
    for start in range(0, near.shape[1], BLOCK):
        part = pl.ds(start, BLOCK)
        value = near[GROUP : 2 * GROUP, part] + near[3 * GROUP : 4 * GROUP, part]
        for m in range(TENORS):
            value = value + pull[m] * tenors[GROUP * m : GROUP * (m + 1), part]
        alloc[:, part] = value
        rounded[:, part] = twice(value)
    sums_by_node(rounded, low_hot, pair_hot, 2 * BUCKETS, keep, send)


def join_kernel(own, keep, more, passed, *chunks):
    passed[...] = own[...]
    size = chunks[0].shape[0]
    for c, chunk in enumerate(chunks):
        part = pl.ds(c * size, size)
        chunk[...] = keep[part] + more[part]


def capital_kernel(
    count, weight, load, total, product, near, tenors, keep, send, mix, capital, *, trades_total, parts
):
    half = keep.shape[0]
    length = product.shape[1] // parts
    gather = total[...]
    lane = lax.broadcasted_iota(jnp.int32, (GROUP, LANES), 1)
    row = lax.broadcasted_iota(jnp.int32, (GROUP, 1), 0)
    real = row < BUCKETS
    risk = jnp.zeros((GROUP, 1), f32)
    loading = jnp.zeros((GROUP, 1), f32)
    for b in range(BUCKETS):
        risk = jnp.where(row == b, weight[b], risk)
        loading = jnp.where(row == b, load[b], loading)
    tenor_part = jnp.where(lane < TENORS, gather, 0.0)
    sums = jnp.sum(tenor_part, 1, keepdims=True)
    tenor_square = jnp.sum(tenor_part * tenor_part, 1, keepdims=True)
    own_square = gather[:, TENORS : TENORS + 1]
    name_square = gather[:, TENORS + 1 : TENORS + 2]
    columns = []
    row8 = lax.broadcasted_iota(jnp.int32, (8, LANES), 0)
    capitals = jnp.zeros((8, LANES), f32)
    for s in range(SCEN):
        level = [float(v) for v in LEVELS[s]]
        form = level[3] * sums * sums + (level[2] - level[3]) * tenor_square
        form = form + (level[1] - level[3]) * name_square + float(SAME_BOTH[s]) * own_square
        root = jnp.sqrt(form + 1e-6)
        radius = jnp.sqrt(root * root + sums * sums)
        capped = sums * root / radius
        pulled = jnp.where(real, loading * capped, 0.0)
        loaded = jnp.sum(pulled, 0, keepdims=True)
        squares = jnp.sum(pulled * pulled, 0, keepdims=True)
        cross = CROSS * SCENARIO[s]
        inside = jnp.sum(jnp.where(real, root * root, 0.0), 0, keepdims=True)
        cap = jnp.sqrt(inside + cross * (loaded * loaded - squares))
        cross_pull = cross * (loading * loaded - loading * loading * capped) / cap
        ratio = sums / radius
        share = root / radius
        coef_form = (root / cap + cross_pull * ratio * ratio * ratio) / root
        coef_sum = cross_pull * share * share * share
        scale = jnp.where(real, risk / cap, 0.0)
        columns.append(
            [
                scale * coef_form * (1.0 - SCENARIO[s]),
                scale * coef_sum,
                scale * coef_form * SCENARIO[s],
            ]
        )
        capitals = jnp.where(row8 == s, cap, capitals)
    capital[...] = capitals
    for s in range(SCEN):
        column = jnp.concatenate([c[:BUCKETS] for c in columns[s]], 0)
        mix[s] = jnp.broadcast_to(column * float(NODES), (3 * BUCKETS, LANES))
    f = lax.axis_index("factor")
    bits = parts.bit_length() - 1
    for p in range(parts):
        block = f ^ sum(((p >> i) & 1) << (bits - 1 - i) for i in range(bits))
        rows = pl.ds(pl.multiple_of(block * length, LANES), length)
        values = [
            near[:GROUP, rows] + near[2 * GROUP : 3 * GROUP, rows],
            tenors[GROUP * (TENORS - 1) : GROUP * TENORS, rows],
            product[:, rows],
        ]
        slot = lax.broadcasted_iota(jnp.int32, (1, BLOCK), 1)
        live = [
            jnp.where(slot < count[block * (length // BLOCK) + i], 1.0, 0.0)
            for i in range(length // BLOCK)
        ]
        live = jnp.concatenate(live, 1)
        for s in range(SCEN):
            out = sum(v * (c * float(trades_total)) for v, c in zip(values, columns[s]))
            out = jnp.sum(out, 0, keepdims=True) * live
            for j in range(length // LANES):
                place = s * (length // LANES) + j
                piece = out[:, j * LANES : (j + 1) * LANES]
                if p < half:
                    keep[p, place : place + 1] = piece
                else:
                    send[p - half, place : place + 1] = piece


def finish_kernel(mix, capital, trade_keep, trade_more, *refs, scale):
    *pieces, scaled, trades, nodes = refs
    total = sum(p[...] for p in pieces)
    for s in range(SCEN):
        mixed = mix[s][:, : total.shape[1]] * total
        nodes[s] = sum(mixed[BUCKETS * j : BUCKETS * (j + 1)] for j in range(3))
    value = trade_keep[...] + trade_more[...]
    count = value.shape[0] // SCEN
    for s in range(SCEN):
        for j in range(count):
            place = s * count + j
            trades[s : s + 1, j * LANES : (j + 1) * LANES] = value[place : place + 1]
    for s in range(SCEN):
        scaled[s] = jnp.max(capital[s : s + 1, :]) * scale


def local(
    sensitivity,
    block_count,
    trade_node,
    factor_bucket,
    risk_weight,
    bucket_loading,
    *,
    trade_size,
    factor_size,
):
    trade_rows, width = sensitivity.shape
    trades_total = trade_rows * trade_size
    devices = trade_size * factor_size
    trade_bits = trade_size.bit_length() - 1
    factor_bits = factor_size.bit_length() - 1
    bits = trade_bits + factor_bits

    def exchange(x, mask):
        return lax.ppermute(x, AXES, [(o, o ^ mask) for o in range(devices)])

    over_factor = list(range(1, factor_bits))
    over_trade = list(range(factor_bits, bits))
    groups = [over_factor[:1] + over_trade[:1], over_trade[1:3]]
    groups += [[b] for b in over_factor[1:] + over_trade[3:]]
    order = [0] + sum(groups, [])
    places = [7, 11, 10, 9, 8, 6, 5, 4, 3, 2, 1, 0]
    spots = [0] * bits
    for i, bit in enumerate(order):
        spots[bit] = 1 << places[i]

    def in_hbm(x):
        return pltpu.with_memory_space_constraint(x, pltpu.HBM)

    rows = pltpu.VMEM((GROUP, trade_rows), f32)
    multiplied = pltpu.VMEM((128, trade_rows), f32)
    rounded = pltpu.VMEM((2 * GROUP, trade_rows), bf16)
    lines = (factor_bucket.shape[0] // LANES, LANES)
    held, raw, low_hot, pair_hot, hot, ones_hot, factor_weight = call(
        functools.partial(totals_kernel, spots=spots, factor_size=factor_size),
        (
            pltpu.VMEM((width, trade_rows), bf16),
            shape(1, width),
            pltpu.VMEM((LOW, trade_rows), bf16),
            pltpu.VMEM((HIGH // 2, 2 * GROUP, trade_rows), bf16),
            pltpu.VMEM((128, width), bf16),
            pltpu.VMEM((128, width), bf16),
            pltpu.VMEM((1, width), f32),
        ),
        [ANY] * 5,
        (VMEM,) * 7,
        "totals",
        scratch=[
            pltpu.SMEM(block_count.shape, jnp.int32),
            pltpu.SMEM(risk_weight.shape, f32),
            pltpu.VMEM((1, trade_rows), jnp.int32),
            pltpu.VMEM(lines, jnp.int32),
            pltpu.VMEM((1, width), jnp.int32),
            pltpu.SemaphoreType.DMA((-(-width // PIECE),)),
            pltpu.SemaphoreType.DMA((4,)),
        ],
        flops=10**7,
    )(
        in_hbm(block_count),
        in_hbm(risk_weight),
        in_hbm(trade_node[None, :]),
        in_hbm(factor_bucket.reshape(lines)),
        in_hbm(sensitivity.T),
    )

    trade_mask = [1 << b for b in over_trade]
    other = exchange(raw, trade_mask[0])
    tenors, ones_rounded, raw = call(
        ones_kernel,
        (multiplied, rounded, shape(1, width)),
        [VMEM] * 3,
        (VMEM,) * 3,
        "ones",
        flops=2 * 128 * width * trade_rows,
    )(raw, ones_hot, held)
    raw = raw + other
    for mask in trade_mask[3:]:
        raw = raw + exchange(raw, mask)
    others = [
        exchange(raw, mask)
        for mask in (trade_mask[1], trade_mask[2], trade_mask[1] + trade_mask[2])
    ]

    all_nodes = (HIGH, 3 * BUCKETS, LOW // 2)
    nodes_flops = 2 * 512 * trade_rows * LOW
    keep, send, raw = call(
        ones_nodes_kernel,
        (pltpu.VMEM(all_nodes, f32), pltpu.VMEM(all_nodes, f32), shape(1, width)),
        [VMEM] * 4,
        (VMEM,) * 3,
        "ones_nodes",
        flops=nodes_flops,
    )(raw, ones_rounded, low_hot, pair_hot)

    spread, sums = call(
        weights_kernel,
        (pltpu.VMEM((128, width), bf16), shape(GROUP, LANES)),
        [VMEM] * (4 + len(others)),
        (VMEM, VMEM),
        "weights",
        flops=10**6,
    )(raw, *others, factor_weight, hot, ones_hot)

    others = [exchange(sums, mask) for mask in range(1, factor_size)]
    near, weighted_rounded = call(
        spread_kernel,
        (multiplied, rounded),
        [VMEM] * 2,
        (VMEM,) * 2,
        "spread",
        flops=2 * 128 * width * trade_rows,
    )(spread, held)
    keep, send = call(
        weighted_nodes_kernel,
        (pltpu.VMEM(all_nodes, f32),) * 2,
        [VMEM] * 5,
        (VMEM,) * 2,
        "weighted_nodes",
        alias={3: 0, 4: 1},
        flops=nodes_flops,
    )(weighted_rounded, low_hot, pair_hot, keep, send)

    product, total, keep, send = call(
        product_nodes_kernel,
        (rows, shape(GROUP, LANES), pltpu.VMEM(all_nodes, f32), pltpu.VMEM(all_nodes, f32)),
        [VMEM] * (7 + len(others)),
        (VMEM,) * 4,
        "product_nodes",
        alias={5 + len(others): 2, 6 + len(others): 3},
        scratch=[rounded],
        flops=nodes_flops,
    )(sums, *others, near, tenors, low_hot, pair_hot, keep, send)
    from_core = exchange(send, 1)

    trade_shape = shape(factor_size // 2, SCEN * trade_rows // factor_size // LANES, LANES)
    trade_keep, trade_send, mix, capital = call(
        functools.partial(capital_kernel, trades_total=trades_total, parts=factor_size),
        (trade_shape, trade_shape, shape(SCEN, 3 * BUCKETS, LANES), shape(8, LANES)),
        [SMEM, SMEM, SMEM] + [VMEM] * 4,
        (VMEM,) * 4,
        "capital",
        flops=10**7,
    )(block_count, risk_weight, bucket_loading, total, product, near, tenors)

    count = 1 << len(groups[0])
    trade_send, *chunks = call(
        join_kernel,
        (trade_shape,) + (shape(HIGH // count, 3 * BUCKETS, LOW // 2),) * count,
        [VMEM] * 3,
        (VMEM,) * (1 + count),
        "join",
        flops=10**6,
    )(trade_send, keep, from_core)
    trade_more = exchange(trade_send, 1)
    for i, group in enumerate(groups):
        count = 1 << len(group)
        if i > 0:
            axis = 0 if keep.shape[0] > 1 else 2
            chunks = jnp.split(keep, count, axis)
        pieces = [chunks[0]]
        for c in range(count - 1, 0, -1):
            part = [b for j, b in enumerate(group) if (c >> (len(group) - 1 - j)) & 1]
            mask = sum(1 << b for b in part)
            message = chunks[c]
            if len(part) == 1 and part[0] in over_factor:
                trade_send, trade_keep = jnp.split(trade_keep + trade_more, 2, 0)[::-1]
                if message.shape[2] == LANES and i > 0:
                    cut = trade_send.shape[0] * trade_send.shape[1]
                    message = jnp.concatenate(
                        [trade_send.reshape(cut, LANES), message.reshape(-1, LANES)], 0
                    )
                    message = exchange(message, mask)
                    trade_more = message[:cut].reshape(trade_send.shape)
                    message = message[cut:].reshape(chunks[c].shape)
                else:
                    trade_more = exchange(trade_send, mask)
                    message = exchange(message, mask)
            else:
                message = exchange(message, mask)
            pieces.append(message)
        if i + 1 < len(groups):
            keep = sum(pieces[1:], pieces[0])
    return call(
        functools.partial(finish_kernel, scale=1.0 / trades_total**0.5),
        (
            shape(SCEN),
            shape(SCEN, trade_rows // factor_size),
            shape(SCEN, BUCKETS, NODES // devices),
        ),
        [VMEM] * (4 + len(pieces)),
        (SMEM, VMEM, VMEM),
        "finish",
        flops=10**6,
    )(mix, capital, trade_keep[0], trade_more[0], *[p[0] for p in pieces])


def solution(mesh):
    sizes = dict(mesh.shape)
    return jax.shard_map(
        functools.partial(local, trade_size=sizes["trade"], factor_size=sizes["factor"]),
        mesh=mesh,
        in_specs=(P("trade", "factor"), P("trade"), P("trade"), P(), P(), P()),
        out_specs=(P(), P(None, ("trade", "factor")), P(None, None, ("trade", "factor"))),
        check_vma=False,
    )
```

```python
import functools

import jax
import jax.numpy as jnp
import numpy as np
from jax import lax
from jax.experimental import pallas as pl
from jax.experimental.pallas import tpu as pltpu
from jax.sharding import PartitionSpec as P

TENORS = 5
BUCKETS = 18
GROUP = 24
SCEN = 3
NODES = 4096
BLOCK = 512
LANES = 128
PIECE = 256
LOW = 256
HIGH = NODES // LOW
AXES = ("trade", "factor")
MIB = 1 << 20

BASE = np.array([1.0, 0.65, 0.35, 0.2275], np.float32)
LEVELS = np.stack([BASE, np.minimum(1.25 * BASE, 1.0), np.maximum(2.0 * BASE - 1.0, 0.75 * BASE)])
SCENARIO = (1.0, 1.25, 0.75)
CROSS = 0.5
SAME_BOTH = LEVELS[:, 0] - LEVELS[:, 1] - LEVELS[:, 2] + LEVELS[:, 3]

SMEM = pl.BlockSpec(memory_space=pltpu.SMEM)
VMEM = pl.BlockSpec(memory_space=pltpu.VMEM)
ANY = pl.BlockSpec(memory_space=pl.ANY)
f32 = jnp.float32
bf16 = jnp.bfloat16


def shape(*dims, dtype=f32):
    return jax.ShapeDtypeStruct(dims, dtype)


def call(kernel, out_shape, in_specs, out_specs, name, scratch=(), flops=0, alias=None, limit=8):
    return pl.pallas_call(
        kernel,
        out_shape=out_shape,
        in_specs=in_specs,
        out_specs=out_specs,
        scratch_shapes=list(scratch),
        name=name,
        input_output_aliases=alias or {},
        compiler_params=pltpu.CompilerParams(vmem_limit_bytes=limit * MIB),
        cost_estimate=pl.CostEstimate(flops=flops, bytes_accessed=1 << 16, transcendentals=0),
    )


def dot(a, b):
    return lax.dot_general(a, b, (((1,), (0,)), ((), ())), preferred_element_type=f32)


def dot_t(a, b):
    return lax.dot_general(a, b, (((1,), (1,)), ((), ())), preferred_element_type=f32)


def three_parts(value):
    upper = value.astype(bf16).astype(f32)
    middle = (value - upper).astype(bf16).astype(f32)
    return upper, middle, value - upper - middle


def fill_tables(
    count, weight, nodes, bucket, low_hot, pair_hot, hot, ones_hot, factor_weight, me, spots
):
    bits = len(spots)
    inner = (NODES >> bits).bit_length() - 1
    node = nodes[...]
    other = (node >> inner) ^ me
    label = node & ((1 << inner) - 1)
    for i in range(bits):
        label = label + ((other >> i) & 1) * spots[i]
    low = label & (LOW - 1)
    high = label >> (LOW.bit_length() - 1)
    for i in range(node.shape[1] // BLOCK):
        part = slice(i * BLOCK, (i + 1) * BLOCK)
        here = lax.broadcasted_iota(jnp.int32, (LOW, BLOCK), 0) == low[:, part]
        low_hot[:, part] = jnp.where(here, 1.0, 0.0).astype(bf16)
        row = lax.broadcasted_iota(jnp.int32, (2 * GROUP, BLOCK), 0)
        away = high[:, part] - jnp.where(row < GROUP, 0, 1)
        slot = lax.broadcasted_iota(jnp.int32, (2 * GROUP, BLOCK), 1)
        away = jnp.where(slot < count[i], away, -1)
        for p in range(HIGH // 2):
            pair_hot[p, :, part] = jnp.where(away == 2 * p, 1.0, 0.0).astype(bf16)
    width = bucket.shape[1]
    column = lax.rem(lax.broadcasted_iota(jnp.int32, (1, width), 1), TENORS)
    row = lax.broadcasted_iota(jnp.int32, (GROUP, width), 0)
    every = row == bucket
    by_tenor = [jnp.where(every & (column == m), 1.0, 0.0) for m in range(TENORS)]
    fill = [jnp.zeros((8, width), f32)]
    hot[...] = jnp.concatenate(by_tenor + fill, 0).astype(bf16)
    every = [jnp.where(every, 1.0, 0.0)]
    ones_hot[...] = jnp.concatenate(by_tenor[:-1] + every + fill, 0).astype(bf16)
    total = jnp.zeros((1, width), f32)
    for b in range(BUCKETS):
        total = jnp.where(bucket == b, weight[b], total)
    factor_weight[...] = total


def totals_kernel(
    count_hbm,
    weight_hbm,
    nodes_hbm,
    buckets_hbm,
    sens,
    held,
    raw,
    low_hot,
    pair_hot,
    hot,
    ones_hot,
    factor_weight,
    count,
    weight,
    nodes,
    buckets,
    bucket,
    sems,
    small_sems,
    *,
    spots,
    factor_size,
):
    width, trades = sens.shape
    pieces = [(start, min(PIECE, width - start)) for start in range(0, width, PIECE)]
    small = []
    for i, (source, target) in enumerate(
        [(count_hbm, count), (weight_hbm, weight), (nodes_hbm, nodes), (buckets_hbm, buckets)]
    ):
        small.append(pltpu.make_async_copy(source, target, small_sems.at[i]))
        small[-1].start()
    copies = []
    for i, (start, rows) in enumerate(pieces):
        part = pl.ds(start, rows)
        copies.append(pltpu.make_async_copy(sens.at[part], held.at[part], sems.at[i]))
    copies[0].start()
    for copy in small:
        copy.wait()
    for copy in copies[1:]:
        copy.start()
    f = lax.axis_index("factor")
    me = lax.axis_index("trade") * factor_size + f
    for i in range(factor_size):

        @pl.when(f == i)
        def _(i=i):
            first, off = divmod(i * width, LANES)
            last = -(-(off + width) // LANES) + first
            row = jnp.concatenate([buckets[r : r + 1] for r in range(first, last)], 1)
            bucket[...] = row[:, off : off + width]

    fill_tables(
        count,
        weight,
        nodes,
        bucket[...],
        low_hot,
        pair_hot,
        hot,
        ones_hot,
        factor_weight,
        me,
        spots,
    )
    ones = jnp.ones((16, 3 * LANES), bf16)

    def run(tiles):
        for copy, (start, rows) in zip(copies, pieces):
            copy.wait()
            chains = 1 if rows > 128 else 4
            totals = [None] * chains
            for i, (lane, live) in enumerate(tiles(rows)):
                part = held[start : start + rows, lane : lane + LANES].astype(f32)
                if live is not None:
                    part = jnp.where(live, part, 0.0)
                j = i % chains
                totals[j] = part if totals[j] is None else totals[j] + part
            value = sum(totals[1:], totals[0])
            parts = jnp.concatenate(three_parts(value), 1).astype(bf16)
            raw[:, start : start + rows] = dot_t(ones, parts)[:1]

    full = count[0] == BLOCK

    @pl.when(full)
    def _():
        run(lambda rows: [(lane, None) for lane in range(0, trades, LANES)])

    @pl.when(jnp.logical_not(full))
    def _():
        def tiles(rows):
            slot = lax.broadcasted_iota(jnp.int32, (rows, LANES), 1)
            return [(i * BLOCK, slot < count[i]) for i in range(trades // BLOCK)]

        run(tiles)


def multiply(weights, held, product):
    for start in range(0, held.shape[1], BLOCK):
        part = pl.ds(start, BLOCK)
        product[:, part] = dot(weights, held[:, part])


def twice(value):
    return jnp.concatenate([value, value], 0).astype(bf16)


def ones_kernel(own, ones_hot, held, product, rounded, passed):
    passed[...] = own[...]
    multiply(ones_hot[...], held, product)
    rounded[...] = twice(product[GROUP * (TENORS - 1) : GROUP * TENORS])


def sums_by_node(rounded, low_hot, pair_hot, first, keep, send):
    value = rounded[...]
    masked = jnp.concatenate([value * pair_hot[p] for p in range(HIGH // 2)], 0)
    out = dot_t(masked, low_hot[...])
    for h in range(HIGH):
        rows = out[GROUP * h : GROUP * h + BUCKETS]
        place = 3 * BUCKETS * h + first
        keep[place : place + BUCKETS] = rows[:, : LOW // 2]
        send[place : place + BUCKETS] = rows[:, LOW // 2 :]


def ones_nodes_kernel(own, rounded, low_hot, pair_hot, keep, send, passed):
    passed[...] = own[...]
    sums_by_node(rounded, low_hot, pair_hot, BUCKETS, keep, send)


def weights_kernel(*refs):
    *raws, factor_weight, hot, ones_hot, spread, sums = refs
    width = factor_weight.shape[1]
    weighted = factor_weight[...] * sum(r[...] for r in raws)
    own_tenor = lax.rem(lax.broadcasted_iota(jnp.int32, (1, width), 1), TENORS)
    name = weighted
    for d in range(1, TENORS):
        zeros = jnp.zeros((1, d), f32)
        after = jnp.concatenate([weighted[:, d:], zeros], 1)
        before = jnp.concatenate([zeros, weighted[:, : width - d]], 1)
        name = name + jnp.where(own_tenor < TENORS - d, after, 0.0)
        name = name + jnp.where(own_tenor >= d, before, 0.0)
    near = float(LEVELS[0, 1] - LEVELS[0, 3]) * name + float(SAME_BOTH[0]) * weighted
    every = ones_hot[GROUP * (TENORS - 1) : GROUP * TENORS].astype(f32)
    full = jnp.concatenate([every * weighted, every * near], 0)
    upper = full.astype(bf16).astype(f32)
    fill = jnp.zeros((32, width), f32)
    spread[...] = jnp.concatenate([upper, full - upper, fill], 0).astype(bf16)
    lane = lax.broadcasted_iota(jnp.int32, (GROUP, LANES), 1)
    square = jnp.sum(every * (weighted * weighted), 1, keepdims=True)
    out = jnp.where(lane == TENORS, square, 0.0)
    first = jnp.where(own_tenor == 0, name, 0.0)
    names = jnp.sum(every * (first * first), 1, keepdims=True)
    out = jnp.where(lane == TENORS + 1, names, out)
    by_tenor = hot[...].astype(f32) * weighted
    for m in range(TENORS):
        part = jnp.sum(by_tenor[GROUP * m : GROUP * (m + 1)], 1, keepdims=True)
        out = jnp.where(lane == m, part, out)
    sums[...] = out


def spread_kernel(spread, held, product, rounded):
    multiply(spread[...], held, product)
    rounded[...] = twice(product[:GROUP] + product[2 * GROUP : 3 * GROUP])


def weighted_nodes_kernel(rounded, low_hot, pair_hot, _, __, keep, send):
    sums_by_node(rounded, low_hot, pair_hot, 0, keep, send)


def product_nodes_kernel(*refs):
    *sums, near, tenors, low_hot, pair_hot, _, _, alloc, total, keep, send, rounded = refs
    gather = sum(r[...] for r in sums)
    total[...] = gather
    lane = lax.broadcasted_iota(jnp.int32, (GROUP, LANES), 1)
    bucket = jnp.sum(jnp.where(lane < TENORS, gather, 0.0), 1, keepdims=True)
    same = float(LEVELS[0, 2] - LEVELS[0, 3])
    last = gather[:, TENORS - 1 : TENORS]
    pull = [same * (gather[:, m : m + 1] - last) for m in range(TENORS - 1)]
    pull.append(same * last + float(LEVELS[0, 3]) * bucket)
    for start in range(0, near.shape[1], BLOCK):
        part = pl.ds(start, BLOCK)
        value = near[GROUP : 2 * GROUP, part] + near[3 * GROUP : 4 * GROUP, part]
        for m in range(TENORS):
            value = value + pull[m] * tenors[GROUP * m : GROUP * (m + 1), part]
        alloc[:, part] = value
        rounded[:, part] = twice(value)
    sums_by_node(rounded, low_hot, pair_hot, 2 * BUCKETS, keep, send)


def join_kernel(own, keep, more, passed, *chunks):
    passed[...] = own[...]
    size = chunks[0].shape[0]
    for c, chunk in enumerate(chunks):
        part = pl.ds(c * size, size)
        chunk[...] = keep[part] + more[part]


def middle_kernel(*refs, count):
    pieces, chunks = refs[:count], refs[count:]
    total = sum(p[...] for p in pieces)
    for c, chunk in enumerate(chunks):
        for j in range(chunk.shape[0]):
            place = 3 * BUCKETS * (c * chunk.shape[0] + j)
            chunk[j] = total[place : place + 3 * BUCKETS]


def capital_kernel(
    count, weight, load, total, product, near, tenors, keep, send, mix, capital, *, trades_total, parts
):
    half = keep.shape[0]
    length = product.shape[1] // parts
    gather = total[...]
    lane = lax.broadcasted_iota(jnp.int32, (GROUP, LANES), 1)
    row = lax.broadcasted_iota(jnp.int32, (GROUP, 1), 0)
    real = row < BUCKETS
    risk = jnp.zeros((GROUP, 1), f32)
    loading = jnp.zeros((GROUP, 1), f32)
    for b in range(BUCKETS):
        risk = jnp.where(row == b, weight[b], risk)
        loading = jnp.where(row == b, load[b], loading)
    tenor_part = jnp.where(lane < TENORS, gather, 0.0)
    sums = jnp.sum(tenor_part, 1, keepdims=True)
    tenor_square = jnp.sum(tenor_part * tenor_part, 1, keepdims=True)
    own_square = gather[:, TENORS : TENORS + 1]
    name_square = gather[:, TENORS + 1 : TENORS + 2]
    columns = []
    row8 = lax.broadcasted_iota(jnp.int32, (8, LANES), 0)
    capitals = jnp.zeros((8, LANES), f32)
    for s in range(SCEN):
        level = [float(v) for v in LEVELS[s]]
        form = level[3] * sums * sums + (level[2] - level[3]) * tenor_square
        form = form + (level[1] - level[3]) * name_square + float(SAME_BOTH[s]) * own_square
        root = jnp.sqrt(form + 1e-6)
        radius = jnp.sqrt(root * root + sums * sums)
        capped = sums * root / radius
        pulled = jnp.where(real, loading * capped, 0.0)
        loaded = jnp.sum(pulled, 0, keepdims=True)
        squares = jnp.sum(pulled * pulled, 0, keepdims=True)
        cross = CROSS * SCENARIO[s]
        inside = jnp.sum(jnp.where(real, root * root, 0.0), 0, keepdims=True)
        cap = jnp.sqrt(inside + cross * (loaded * loaded - squares))
        cross_pull = cross * (loading * loaded - loading * loading * capped) / cap
        ratio = sums / radius
        share = root / radius
        coef_form = (root / cap + cross_pull * ratio * ratio * ratio) / root
        coef_sum = cross_pull * share * share * share
        scale = jnp.where(real, risk / cap, 0.0)
        columns.append(
            [
                scale * coef_form * (1.0 - SCENARIO[s]),
                scale * coef_sum,
                scale * coef_form * SCENARIO[s],
            ]
        )
        capitals = jnp.where(row8 == s, cap, capitals)
    capital[...] = capitals
    for s in range(SCEN):
        column = jnp.concatenate([c[:BUCKETS] for c in columns[s]], 0)
        mix[s] = jnp.broadcast_to(column * float(NODES), (3 * BUCKETS, LANES))
    f = lax.axis_index("factor")
    bits = parts.bit_length() - 1
    for p in range(parts):
        block = f ^ sum(((p >> i) & 1) << (bits - 1 - i) for i in range(bits))
        rows = pl.ds(pl.multiple_of(block * length, LANES), length)
        values = [
            near[:GROUP, rows] + near[2 * GROUP : 3 * GROUP, rows],
            tenors[GROUP * (TENORS - 1) : GROUP * TENORS, rows],
            product[:, rows],
        ]
        slot = lax.broadcasted_iota(jnp.int32, (1, BLOCK), 1)
        live = [
            jnp.where(slot < count[block * (length // BLOCK) + i], 1.0, 0.0)
            for i in range(length // BLOCK)
        ]
        live = jnp.concatenate(live, 1)
        for s in range(SCEN):
            out = sum(v * (c * float(trades_total)) for v, c in zip(values, columns[s]))
            out = jnp.sum(out, 0, keepdims=True) * live
            for j in range(length // LANES):
                place = s * (length // LANES) + j
                piece = out[:, j * LANES : (j + 1) * LANES]
                if p < half:
                    keep[p, place : place + 1] = piece
                else:
                    send[p - half, place : place + 1] = piece


def finish_kernel(mix, capital, trade_keep, trade_more, *refs, scale):
    *pieces, scaled, trades, nodes = refs
    total = sum(p[...] for p in pieces)
    for s in range(SCEN):
        mixed = mix[s][:, : total.shape[1]] * total
        nodes[s] = sum(mixed[BUCKETS * j : BUCKETS * (j + 1)] for j in range(3))
    value = trade_keep[...] + trade_more[...]
    count = value.shape[0] // SCEN
    for s in range(SCEN):
        for j in range(count):
            place = s * count + j
            trades[s : s + 1, j * LANES : (j + 1) * LANES] = value[place : place + 1]
    for s in range(SCEN):
        scaled[s] = jnp.max(capital[s : s + 1, :]) * scale


def local(
    sensitivity,
    block_count,
    trade_node,
    factor_bucket,
    risk_weight,
    bucket_loading,
    *,
    trade_size,
    factor_size,
):
    trade_rows, width = sensitivity.shape
    trades_total = trade_rows * trade_size
    devices = trade_size * factor_size
    trade_bits = trade_size.bit_length() - 1
    factor_bits = factor_size.bit_length() - 1
    bits = trade_bits + factor_bits

    def exchange(x, mask):
        return lax.ppermute(x, AXES, [(o, o ^ mask) for o in range(devices)])

    over_factor = list(range(1, factor_bits))
    over_trade = list(range(factor_bits, bits))
    groups = [over_factor[:1] + over_trade[:1], over_trade[1:3]]
    groups += [[b] for b in over_factor[1:] + over_trade[3:]]
    order = [0] + sum(groups, [])
    places = [7, 11, 10, 9, 8, 6, 5, 4, 3, 2, 1, 0]
    spots = [0] * bits
    for i, bit in enumerate(order):
        spots[bit] = 1 << places[i]

    def in_hbm(x):
        return pltpu.with_memory_space_constraint(x, pltpu.HBM)

    rows = pltpu.VMEM((GROUP, trade_rows), f32)
    multiplied = pltpu.VMEM((128, trade_rows), f32)
    rounded = pltpu.VMEM((2 * GROUP, trade_rows), bf16)
    lines = (factor_bucket.shape[0] // LANES, LANES)
    held, raw, low_hot, pair_hot, hot, ones_hot, factor_weight = call(
        functools.partial(totals_kernel, spots=spots, factor_size=factor_size),
        (
            pltpu.VMEM((width, trade_rows), bf16),
            shape(1, width),
            pltpu.VMEM((LOW, trade_rows), bf16),
            pltpu.VMEM((HIGH // 2, 2 * GROUP, trade_rows), bf16),
            pltpu.VMEM((128, width), bf16),
            pltpu.VMEM((128, width), bf16),
            pltpu.VMEM((1, width), f32),
        ),
        [ANY] * 5,
        (VMEM,) * 7,
        "totals",
        scratch=[
            pltpu.SMEM(block_count.shape, jnp.int32),
            pltpu.SMEM(risk_weight.shape, f32),
            pltpu.VMEM((1, trade_rows), jnp.int32),
            pltpu.VMEM(lines, jnp.int32),
            pltpu.VMEM((1, width), jnp.int32),
            pltpu.SemaphoreType.DMA((-(-width // PIECE),)),
            pltpu.SemaphoreType.DMA((4,)),
        ],
        flops=10**7,
    )(
        in_hbm(block_count),
        in_hbm(risk_weight),
        in_hbm(trade_node[None, :]),
        in_hbm(factor_bucket.reshape(lines)),
        in_hbm(sensitivity.T),
    )

    trade_mask = [1 << b for b in over_trade]
    other = exchange(raw, trade_mask[0])
    tenors, ones_rounded, raw = call(
        ones_kernel,
        (multiplied, rounded, shape(1, width)),
        [VMEM] * 3,
        (VMEM,) * 3,
        "ones",
        flops=2 * 128 * width * trade_rows,
    )(raw, ones_hot, held)
    raw = raw + other
    for mask in trade_mask[3:]:
        raw = raw + exchange(raw, mask)
    others = [
        exchange(raw, mask)
        for mask in (trade_mask[1], trade_mask[2], trade_mask[1] + trade_mask[2])
    ]

    all_nodes = (HIGH * 3 * BUCKETS, LOW // 2)
    nodes_flops = 2 * 512 * trade_rows * LOW
    keep, send, raw = call(
        ones_nodes_kernel,
        (pltpu.VMEM(all_nodes, f32), pltpu.VMEM(all_nodes, f32), shape(1, width)),
        [VMEM] * 4,
        (VMEM,) * 3,
        "ones_nodes",
        flops=nodes_flops,
    )(raw, ones_rounded, low_hot, pair_hot)

    spread, sums = call(
        weights_kernel,
        (pltpu.VMEM((128, width), bf16), shape(GROUP, LANES)),
        [VMEM] * (4 + len(others)),
        (VMEM, VMEM),
        "weights",
        flops=10**6,
    )(raw, *others, factor_weight, hot, ones_hot)

    others = [exchange(sums, mask) for mask in range(1, factor_size)]
    near, weighted_rounded = call(
        spread_kernel,
        (multiplied, rounded),
        [VMEM] * 2,
        (VMEM,) * 2,
        "spread",
        flops=2 * 128 * width * trade_rows,
    )(spread, held)
    keep, send = call(
        weighted_nodes_kernel,
        (pltpu.VMEM(all_nodes, f32),) * 2,
        [VMEM] * 5,
        (VMEM,) * 2,
        "weighted_nodes",
        alias={3: 0, 4: 1},
        flops=nodes_flops,
    )(weighted_rounded, low_hot, pair_hot, keep, send)

    product, total, keep, send = call(
        product_nodes_kernel,
        (rows, shape(GROUP, LANES), pltpu.VMEM(all_nodes, f32), pltpu.VMEM(all_nodes, f32)),
        [VMEM] * (7 + len(others)),
        (VMEM,) * 4,
        "product_nodes",
        alias={5 + len(others): 2, 6 + len(others): 3},
        scratch=[rounded],
        flops=nodes_flops,
    )(sums, *others, near, tenors, low_hot, pair_hot, keep, send)
    from_core = exchange(send, 1)

    trade_shape = shape(factor_size // 2, SCEN * trade_rows // factor_size // LANES, LANES)
    trade_keep, trade_send, mix, capital = call(
        functools.partial(capital_kernel, trades_total=trades_total, parts=factor_size),
        (trade_shape, trade_shape, shape(SCEN, 3 * BUCKETS, LANES), shape(8, LANES)),
        [SMEM, SMEM, SMEM] + [VMEM] * 4,
        (VMEM,) * 4,
        "capital",
        flops=10**7,
    )(block_count, risk_weight, bucket_loading, total, product, near, tenors)

    count = 1 << len(groups[0])
    trade_send, *chunks = call(
        join_kernel,
        (trade_shape,) + (shape(HIGH // count * 3 * BUCKETS, LOW // 2),) * count,
        [VMEM] * 3,
        (VMEM,) * (1 + count),
        "join",
        flops=10**6,
    )(trade_send, keep, from_core)
    trade_more = exchange(trade_send, 1)
    for i, group in enumerate(groups):
        count = 1 << len(group)
        if i > 1:
            axis = 0 if keep.shape[0] > 1 else 2
            chunks = jnp.split(keep, count, axis)
        pieces = [chunks[0]]
        for c in range(count - 1, 0, -1):
            part = [b for j, b in enumerate(group) if (c >> (len(group) - 1 - j)) & 1]
            mask = sum(1 << b for b in part)
            message = chunks[c]
            if len(part) == 1 and part[0] in over_factor:
                trade_send, trade_keep = jnp.split(trade_keep + trade_more, 2, 0)[::-1]
                if i > 0 and message.shape[2] == LANES:
                    cut = trade_send.shape[0] * trade_send.shape[1]
                    message = jnp.concatenate(
                        [trade_send.reshape(cut, LANES), message.reshape(-1, LANES)], 0
                    )
                    message = exchange(message, mask)
                    trade_more = message[:cut].reshape(trade_send.shape)
                    message = message[cut:].reshape(chunks[c].shape)
                else:
                    trade_more = exchange(trade_send, mask)
                    message = exchange(message, mask)
            else:
                message = exchange(message, mask)
            pieces.append(message)
        if i == 0:
            next_count = 1 << len(groups[1])
            chunk = shape(HIGH // count // next_count, 3 * BUCKETS, LANES)
            chunks = call(
                functools.partial(middle_kernel, count=count),
                (chunk,) * next_count,
                [VMEM] * count,
                (VMEM,) * next_count,
                "middle",
                flops=10**6,
            )(*pieces)
        elif i + 1 < len(groups):
            keep = sum(pieces[1:], pieces[0])
    return call(
        functools.partial(finish_kernel, scale=1.0 / trades_total**0.5),
        (
            shape(SCEN),
            shape(SCEN, trade_rows // factor_size),
            shape(SCEN, BUCKETS, NODES // devices),
        ),
        [VMEM] * (4 + len(pieces)),
        (SMEM, VMEM, VMEM),
        "finish",
        flops=10**6,
    )(mix, capital, trade_keep[0], trade_more[0], *[p[0] for p in pieces])


def solution(mesh):
    sizes = dict(mesh.shape)
    return jax.shard_map(
        functools.partial(local, trade_size=sizes["trade"], factor_size=sizes["factor"]),
        mesh=mesh,
        in_specs=(P("trade", "factor"), P("trade"), P("trade"), P(), P(), P()),
        out_specs=(P(), P(None, ("trade", "factor")), P(None, None, ("trade", "factor"))),
        check_vma=False,
    )
```

```python
import functools

import jax
import jax.numpy as jnp
import numpy as np
from jax import lax
from jax.experimental import pallas as pl
from jax.experimental.pallas import tpu as pltpu
from jax.sharding import PartitionSpec as P

TENORS = 5
BUCKETS = 18
GROUP = 24
SCEN = 3
NODES = 4096
BLOCK = 512
LANES = 128
PIECE = 256
LOW = 256
HIGH = NODES // LOW
AXES = ("trade", "factor")
MIB = 1 << 20

BASE = np.array([1.0, 0.65, 0.35, 0.2275], np.float32)
LEVELS = np.stack([BASE, np.minimum(1.25 * BASE, 1.0), np.maximum(2.0 * BASE - 1.0, 0.75 * BASE)])
SCENARIO = (1.0, 1.25, 0.75)
CROSS = 0.5
SAME_BOTH = LEVELS[:, 0] - LEVELS[:, 1] - LEVELS[:, 2] + LEVELS[:, 3]

SMEM = pl.BlockSpec(memory_space=pltpu.SMEM)
VMEM = pl.BlockSpec(memory_space=pltpu.VMEM)
ANY = pl.BlockSpec(memory_space=pl.ANY)
f32 = jnp.float32
bf16 = jnp.bfloat16


def shape(*dims, dtype=f32):
    return jax.ShapeDtypeStruct(dims, dtype)


def call(kernel, out_shape, in_specs, out_specs, name, scratch=(), flops=0, alias=None, limit=8):
    return pl.pallas_call(
        kernel,
        out_shape=out_shape,
        in_specs=in_specs,
        out_specs=out_specs,
        scratch_shapes=list(scratch),
        name=name,
        input_output_aliases=alias or {},
        compiler_params=pltpu.CompilerParams(vmem_limit_bytes=limit * MIB),
        cost_estimate=pl.CostEstimate(flops=flops, bytes_accessed=1 << 16, transcendentals=0),
    )


def dot(a, b):
    return lax.dot_general(a, b, (((1,), (0,)), ((), ())), preferred_element_type=f32)


def dot_t(a, b):
    return lax.dot_general(a, b, (((1,), (1,)), ((), ())), preferred_element_type=f32)


def three_parts(value):
    upper = value.astype(bf16).astype(f32)
    middle = (value - upper).astype(bf16).astype(f32)
    return upper, middle, value - upper - middle


def fill_labels(count, nodes, low_hot, pair_hot, me, spots):
    bits = len(spots)
    inner = (NODES >> bits).bit_length() - 1
    node = nodes[...]
    other = (node >> inner) ^ me
    label = node & ((1 << inner) - 1)
    for i in range(bits):
        label = label + ((other >> i) & 1) * spots[i]
    low = label & (LOW - 1)
    high = label >> (LOW.bit_length() - 1)
    for i in range(node.shape[1] // BLOCK):
        part = slice(i * BLOCK, (i + 1) * BLOCK)
        here = lax.broadcasted_iota(jnp.int32, (LOW, BLOCK), 0) == low[:, part]
        low_hot[:, part] = jnp.where(here, 1.0, 0.0).astype(bf16)
        row = lax.broadcasted_iota(jnp.int32, (2 * GROUP, BLOCK), 0)
        away = high[:, part] - jnp.where(row < GROUP, 0, 1)
        slot = lax.broadcasted_iota(jnp.int32, (2 * GROUP, BLOCK), 1)
        away = jnp.where(slot < count[i], away, -1)
        for p in range(HIGH // 2):
            pair_hot[p, :, part] = jnp.where(away == 2 * p, 1.0, 0.0).astype(bf16)


def fill_buckets(weight, bucket, hot, ones_hot, factor_weight):
    width = bucket.shape[1]
    column = lax.rem(lax.broadcasted_iota(jnp.int32, (1, width), 1), TENORS)
    row = lax.broadcasted_iota(jnp.int32, (GROUP, width), 0)
    every = row == bucket
    by_tenor = [jnp.where(every & (column == m), 1.0, 0.0) for m in range(TENORS)]
    fill = [jnp.zeros((8, width), f32)]
    hot[...] = jnp.concatenate(by_tenor + fill, 0).astype(bf16)
    every = [jnp.where(every, 1.0, 0.0)]
    ones_hot[...] = jnp.concatenate(by_tenor[:-1] + every + fill, 0).astype(bf16)
    total = jnp.zeros((1, width), f32)
    for b in range(BUCKETS):
        total = jnp.where(bucket == b, weight[b], total)
    factor_weight[...] = total


def totals_kernel(
    count_hbm,
    weight_hbm,
    buckets_hbm,
    sens,
    held,
    raw,
    hot,
    ones_hot,
    factor_weight,
    count,
    weight,
    buckets,
    bucket,
    sems,
    small_sems,
    *,
    factor_size,
):
    width, trades = sens.shape
    pieces = [(start, min(PIECE, width - start)) for start in range(0, width, PIECE)]
    small = []
    for i, (source, target) in enumerate(
        [(count_hbm, count), (weight_hbm, weight), (buckets_hbm, buckets)]
    ):
        small.append(pltpu.make_async_copy(source, target, small_sems.at[i]))
        small[-1].start()
    copies = []
    for i, (start, rows) in enumerate(pieces):
        part = pl.ds(start, rows)
        copies.append(pltpu.make_async_copy(sens.at[part], held.at[part], sems.at[i]))
    copies[0].start()
    for copy in small:
        copy.wait()
    for copy in copies[1:]:
        copy.start()
    f = lax.axis_index("factor")
    for i in range(factor_size):

        @pl.when(f == i)
        def _(i=i):
            first, off = divmod(i * width, LANES)
            last = -(-(off + width) // LANES) + first
            row = jnp.concatenate([buckets[r : r + 1] for r in range(first, last)], 1)
            bucket[...] = row[:, off : off + width]

    fill_buckets(weight, bucket[...], hot, ones_hot, factor_weight)
    ones = jnp.ones((16, 3 * LANES), bf16)

    def run(tiles):
        for copy, (start, rows) in zip(copies, pieces):
            copy.wait()
            chains = 1 if rows > 128 else 4
            totals = [None] * chains
            for i, (lane, live) in enumerate(tiles(rows)):
                part = held[start : start + rows, lane : lane + LANES].astype(f32)
                if live is not None:
                    part = jnp.where(live, part, 0.0)
                j = i % chains
                totals[j] = part if totals[j] is None else totals[j] + part
            value = sum(totals[1:], totals[0])
            parts = jnp.concatenate(three_parts(value), 1).astype(bf16)
            raw[:, start : start + rows] = dot_t(ones, parts)[:1]

    full = count[0] == BLOCK

    @pl.when(full)
    def _():
        run(lambda rows: [(lane, None) for lane in range(0, trades, LANES)])

    @pl.when(jnp.logical_not(full))
    def _():
        def tiles(rows):
            slot = lax.broadcasted_iota(jnp.int32, (rows, LANES), 1)
            return [(i * BLOCK, slot < count[i]) for i in range(trades // BLOCK)]

        run(tiles)


def multiply(weights, held, product):
    for start in range(0, held.shape[1], BLOCK):
        part = pl.ds(start, BLOCK)
        product[:, part] = dot(weights, held[:, part])


def twice(value):
    return jnp.concatenate([value, value], 0).astype(bf16)


def ones_kernel(own, ones_hot, held, product, rounded, passed):
    passed[...] = own[...]
    multiply(ones_hot[...], held, product)
    rounded[...] = twice(product[GROUP * (TENORS - 1) : GROUP * TENORS])


def sums_by_node(rounded, low_hot, pair_hot, first, keep, send):
    value = rounded[...]
    masked = jnp.concatenate([value * pair_hot[p] for p in range(HIGH // 2)], 0)
    out = dot_t(masked, low_hot[...])
    for h in range(HIGH):
        rows = out[GROUP * h : GROUP * h + BUCKETS]
        place = 3 * BUCKETS * h + first
        keep[place : place + BUCKETS] = rows[:, : LOW // 2]
        send[place : place + BUCKETS] = rows[:, LOW // 2 :]


def ones_nodes_kernel(
    count, own, nodes, rounded, low_hot, pair_hot, keep, send, passed, *, spots, factor_size
):
    passed[...] = own[...]
    me = lax.axis_index("trade") * factor_size + lax.axis_index("factor")
    fill_labels(count, nodes, low_hot, pair_hot, me, spots)
    sums_by_node(rounded, low_hot, pair_hot, BUCKETS, keep, send)


def weights_kernel(*refs):
    *raws, factor_weight, hot, ones_hot, spread, sums = refs
    width = factor_weight.shape[1]
    weighted = factor_weight[...] * sum(r[...] for r in raws)
    own_tenor = lax.rem(lax.broadcasted_iota(jnp.int32, (1, width), 1), TENORS)
    name = weighted
    for d in range(1, TENORS):
        zeros = jnp.zeros((1, d), f32)
        after = jnp.concatenate([weighted[:, d:], zeros], 1)
        before = jnp.concatenate([zeros, weighted[:, : width - d]], 1)
        name = name + jnp.where(own_tenor < TENORS - d, after, 0.0)
        name = name + jnp.where(own_tenor >= d, before, 0.0)
    near = float(LEVELS[0, 1] - LEVELS[0, 3]) * name + float(SAME_BOTH[0]) * weighted
    every = ones_hot[GROUP * (TENORS - 1) : GROUP * TENORS].astype(f32)
    full = jnp.concatenate([every * weighted, every * near], 0)
    upper = full.astype(bf16).astype(f32)
    fill = jnp.zeros((32, width), f32)
    spread[...] = jnp.concatenate([upper, full - upper, fill], 0).astype(bf16)
    lane = lax.broadcasted_iota(jnp.int32, (GROUP, LANES), 1)
    square = jnp.sum(every * (weighted * weighted), 1, keepdims=True)
    out = jnp.where(lane == TENORS, square, 0.0)
    first = jnp.where(own_tenor == 0, name, 0.0)
    names = jnp.sum(every * (first * first), 1, keepdims=True)
    out = jnp.where(lane == TENORS + 1, names, out)
    by_tenor = hot[...].astype(f32) * weighted
    for m in range(TENORS):
        part = jnp.sum(by_tenor[GROUP * m : GROUP * (m + 1)], 1, keepdims=True)
        out = jnp.where(lane == m, part, out)
    sums[...] = out


def spread_kernel(spread, held, product, rounded):
    multiply(spread[...], held, product)
    rounded[...] = twice(product[:GROUP] + product[2 * GROUP : 3 * GROUP])


def weighted_nodes_kernel(rounded, low_hot, pair_hot, _, __, keep, send):
    sums_by_node(rounded, low_hot, pair_hot, 0, keep, send)


def product_nodes_kernel(*refs):
    *sums, near, tenors, low_hot, pair_hot, _, _, alloc, total, keep, send, rounded = refs
    gather = sum(r[...] for r in sums)
    total[...] = gather
    lane = lax.broadcasted_iota(jnp.int32, (GROUP, LANES), 1)
    bucket = jnp.sum(jnp.where(lane < TENORS, gather, 0.0), 1, keepdims=True)
    same = float(LEVELS[0, 2] - LEVELS[0, 3])
    last = gather[:, TENORS - 1 : TENORS]
    pull = [same * (gather[:, m : m + 1] - last) for m in range(TENORS - 1)]
    pull.append(same * last + float(LEVELS[0, 3]) * bucket)
    for start in range(0, near.shape[1], BLOCK):
        part = pl.ds(start, BLOCK)
        value = near[GROUP : 2 * GROUP, part] + near[3 * GROUP : 4 * GROUP, part]
        for m in range(TENORS):
            value = value + pull[m] * tenors[GROUP * m : GROUP * (m + 1), part]
        alloc[:, part] = value
        rounded[:, part] = twice(value)
    sums_by_node(rounded, low_hot, pair_hot, 2 * BUCKETS, keep, send)


def join_kernel(own, keep, more, passed, *chunks):
    passed[...] = own[...]
    size = chunks[0].shape[0]
    for c, chunk in enumerate(chunks):
        part = pl.ds(c * size, size)
        chunk[...] = keep[part] + more[part]


def middle_kernel(*refs, count):
    pieces, chunks = refs[:count], refs[count:]
    total = sum(p[...] for p in pieces)
    for c, chunk in enumerate(chunks):
        for j in range(chunk.shape[0]):
            place = 3 * BUCKETS * (c * chunk.shape[0] + j)
            chunk[j] = total[place : place + 3 * BUCKETS]


def capital_kernel(
    count, weight, load, total, product, near, tenors, keep, send, mix, capital, *, trades_total, parts
):
    half = keep.shape[0]
    length = product.shape[1] // parts
    gather = total[...]
    lane = lax.broadcasted_iota(jnp.int32, (GROUP, LANES), 1)
    row = lax.broadcasted_iota(jnp.int32, (GROUP, 1), 0)
    real = row < BUCKETS
    risk = jnp.zeros((GROUP, 1), f32)
    loading = jnp.zeros((GROUP, 1), f32)
    for b in range(BUCKETS):
        risk = jnp.where(row == b, weight[b], risk)
        loading = jnp.where(row == b, load[b], loading)
    tenor_part = jnp.where(lane < TENORS, gather, 0.0)
    sums = jnp.sum(tenor_part, 1, keepdims=True)
    tenor_square = jnp.sum(tenor_part * tenor_part, 1, keepdims=True)
    own_square = gather[:, TENORS : TENORS + 1]
    name_square = gather[:, TENORS + 1 : TENORS + 2]
    columns = []
    row8 = lax.broadcasted_iota(jnp.int32, (8, LANES), 0)
    capitals = jnp.zeros((8, LANES), f32)
    for s in range(SCEN):
        level = [float(v) for v in LEVELS[s]]
        form = level[3] * sums * sums + (level[2] - level[3]) * tenor_square
        form = form + (level[1] - level[3]) * name_square + float(SAME_BOTH[s]) * own_square
        root = jnp.sqrt(form + 1e-6)
        radius = jnp.sqrt(root * root + sums * sums)
        capped = sums * root / radius
        pulled = jnp.where(real, loading * capped, 0.0)
        loaded = jnp.sum(pulled, 0, keepdims=True)
        squares = jnp.sum(pulled * pulled, 0, keepdims=True)
        cross = CROSS * SCENARIO[s]
        inside = jnp.sum(jnp.where(real, root * root, 0.0), 0, keepdims=True)
        cap = jnp.sqrt(inside + cross * (loaded * loaded - squares))
        cross_pull = cross * (loading * loaded - loading * loading * capped) / cap
        ratio = sums / radius
        share = root / radius
        coef_form = (root / cap + cross_pull * ratio * ratio * ratio) / root
        coef_sum = cross_pull * share * share * share
        scale = jnp.where(real, risk / cap, 0.0)
        columns.append(
            [
                scale * coef_form * (1.0 - SCENARIO[s]),
                scale * coef_sum,
                scale * coef_form * SCENARIO[s],
            ]
        )
        capitals = jnp.where(row8 == s, cap, capitals)
    capital[...] = capitals
    for s in range(SCEN):
        column = jnp.concatenate([c[:BUCKETS] for c in columns[s]], 0)
        mix[s] = jnp.broadcast_to(column * float(NODES), (3 * BUCKETS, LANES))
    f = lax.axis_index("factor")
    bits = parts.bit_length() - 1
    for p in range(parts):
        block = f ^ sum(((p >> i) & 1) << (bits - 1 - i) for i in range(bits))
        rows = pl.ds(pl.multiple_of(block * length, LANES), length)
        values = [
            near[:GROUP, rows] + near[2 * GROUP : 3 * GROUP, rows],
            tenors[GROUP * (TENORS - 1) : GROUP * TENORS, rows],
            product[:, rows],
        ]
        slot = lax.broadcasted_iota(jnp.int32, (1, BLOCK), 1)
        live = [
            jnp.where(slot < count[block * (length // BLOCK) + i], 1.0, 0.0)
            for i in range(length // BLOCK)
        ]
        live = jnp.concatenate(live, 1)
        for s in range(SCEN):
            out = sum(v * (c * float(trades_total)) for v, c in zip(values, columns[s]))
            out = jnp.sum(out, 0, keepdims=True) * live
            for j in range(length // LANES):
                place = s * (length // LANES) + j
                piece = out[:, j * LANES : (j + 1) * LANES]
                if p < half:
                    keep[p, place : place + 1] = piece
                else:
                    send[p - half, place : place + 1] = piece


def finish_kernel(mix, capital, trade_keep, trade_more, *refs, scale):
    *pieces, scaled, trades, nodes = refs
    total = sum(p[...] for p in pieces)
    for s in range(SCEN):
        mixed = mix[s][:, : total.shape[1]] * total
        nodes[s] = sum(mixed[BUCKETS * j : BUCKETS * (j + 1)] for j in range(3))
    value = trade_keep[...] + trade_more[...]
    count = value.shape[0] // SCEN
    for s in range(SCEN):
        for j in range(count):
            place = s * count + j
            trades[s : s + 1, j * LANES : (j + 1) * LANES] = value[place : place + 1]
    for s in range(SCEN):
        scaled[s] = jnp.max(capital[s : s + 1, :]) * scale


def local(
    sensitivity,
    block_count,
    trade_node,
    factor_bucket,
    risk_weight,
    bucket_loading,
    *,
    trade_size,
    factor_size,
):
    trade_rows, width = sensitivity.shape
    trades_total = trade_rows * trade_size
    devices = trade_size * factor_size
    trade_bits = trade_size.bit_length() - 1
    factor_bits = factor_size.bit_length() - 1
    bits = trade_bits + factor_bits

    def exchange(x, mask):
        return lax.ppermute(x, AXES, [(o, o ^ mask) for o in range(devices)])

    over_factor = list(range(1, factor_bits))
    over_trade = list(range(factor_bits, bits))
    groups = [over_factor[:1] + over_trade[:1], over_trade[1:3]]
    groups += [[b] for b in over_factor[1:] + over_trade[3:]]
    order = [0] + sum(groups, [])
    places = [7, 11, 10, 9, 8, 6, 5, 4, 3, 2, 1, 0]
    spots = [0] * bits
    for i, bit in enumerate(order):
        spots[bit] = 1 << places[i]

    def in_hbm(x):
        return pltpu.with_memory_space_constraint(x, pltpu.HBM)

    rows = pltpu.VMEM((GROUP, trade_rows), f32)
    multiplied = pltpu.VMEM((128, trade_rows), f32)
    rounded = pltpu.VMEM((2 * GROUP, trade_rows), bf16)
    lines = (factor_bucket.shape[0] // LANES, LANES)
    held, raw, hot, ones_hot, factor_weight = call(
        functools.partial(totals_kernel, factor_size=factor_size),
        (
            pltpu.VMEM((width, trade_rows), bf16),
            shape(1, width),
            pltpu.VMEM((128, width), bf16),
            pltpu.VMEM((128, width), bf16),
            pltpu.VMEM((1, width), f32),
        ),
        [ANY] * 4,
        (VMEM,) * 5,
        "totals",
        scratch=[
            pltpu.SMEM(block_count.shape, jnp.int32),
            pltpu.SMEM(risk_weight.shape, f32),
            pltpu.VMEM(lines, jnp.int32),
            pltpu.VMEM((1, width), jnp.int32),
            pltpu.SemaphoreType.DMA((-(-width // PIECE),)),
            pltpu.SemaphoreType.DMA((3,)),
        ],
        flops=10**7,
    )(
        in_hbm(block_count),
        in_hbm(risk_weight),
        in_hbm(factor_bucket.reshape(lines)),
        in_hbm(sensitivity.T),
    )

    trade_mask = [1 << b for b in over_trade]
    other = exchange(raw, trade_mask[0])
    tenors, ones_rounded, raw = call(
        ones_kernel,
        (multiplied, rounded, shape(1, width)),
        [VMEM] * 3,
        (VMEM,) * 3,
        "ones",
        flops=2 * 128 * width * trade_rows,
    )(raw, ones_hot, held)
    raw = raw + other
    for mask in trade_mask[3:]:
        raw = raw + exchange(raw, mask)
    others = [
        exchange(raw, mask)
        for mask in (trade_mask[1], trade_mask[2], trade_mask[1] + trade_mask[2])
    ]

    all_nodes = (HIGH * 3 * BUCKETS, LOW // 2)
    nodes_flops = 2 * 512 * trade_rows * LOW
    low_hot, pair_hot, keep, send, raw = call(
        functools.partial(ones_nodes_kernel, spots=spots, factor_size=factor_size),
        (
            pltpu.VMEM((LOW, trade_rows), bf16),
            pltpu.VMEM((HIGH // 2, 2 * GROUP, trade_rows), bf16),
            pltpu.VMEM(all_nodes, f32),
            pltpu.VMEM(all_nodes, f32),
            shape(1, width),
        ),
        [SMEM] + [VMEM] * 3,
        (VMEM,) * 5,
        "ones_nodes",
        flops=nodes_flops,
    )(block_count, raw, trade_node[None, :], ones_rounded)

    spread, sums = call(
        weights_kernel,
        (pltpu.VMEM((128, width), bf16), shape(GROUP, LANES)),
        [VMEM] * (4 + len(others)),
        (VMEM, VMEM),
        "weights",
        flops=10**6,
    )(raw, *others, factor_weight, hot, ones_hot)

    others = [exchange(sums, mask) for mask in range(1, factor_size)]
    near, weighted_rounded = call(
        spread_kernel,
        (multiplied, rounded),
        [VMEM] * 2,
        (VMEM,) * 2,
        "spread",
        flops=2 * 128 * width * trade_rows,
    )(spread, held)
    keep, send = call(
        weighted_nodes_kernel,
        (pltpu.VMEM(all_nodes, f32),) * 2,
        [VMEM] * 5,
        (VMEM,) * 2,
        "weighted_nodes",
        alias={3: 0, 4: 1},
        flops=nodes_flops,
    )(weighted_rounded, low_hot, pair_hot, keep, send)

    product, total, keep, send = call(
        product_nodes_kernel,
        (rows, shape(GROUP, LANES), pltpu.VMEM(all_nodes, f32), pltpu.VMEM(all_nodes, f32)),
        [VMEM] * (7 + len(others)),
        (VMEM,) * 4,
        "product_nodes",
        alias={5 + len(others): 2, 6 + len(others): 3},
        scratch=[rounded],
        flops=nodes_flops,
    )(sums, *others, near, tenors, low_hot, pair_hot, keep, send)
    from_core = exchange(send, 1)

    trade_shape = shape(factor_size // 2, SCEN * trade_rows // factor_size // LANES, LANES)
    trade_keep, trade_send, mix, capital = call(
        functools.partial(capital_kernel, trades_total=trades_total, parts=factor_size),
        (trade_shape, trade_shape, shape(SCEN, 3 * BUCKETS, LANES), shape(8, LANES)),
        [SMEM, SMEM, SMEM] + [VMEM] * 4,
        (VMEM,) * 4,
        "capital",
        flops=10**7,
    )(block_count, risk_weight, bucket_loading, total, product, near, tenors)

    count = 1 << len(groups[0])
    trade_send, *chunks = call(
        join_kernel,
        (trade_shape,) + (shape(HIGH // count * 3 * BUCKETS, LOW // 2),) * count,
        [VMEM] * 3,
        (VMEM,) * (1 + count),
        "join",
        flops=10**6,
    )(trade_send, keep, from_core)
    trade_more = exchange(trade_send, 1)
    for i, group in enumerate(groups):
        count = 1 << len(group)
        if i > 1:
            axis = 0 if keep.shape[0] > 1 else 2
            chunks = jnp.split(keep, count, axis)
        pieces = [chunks[0]]
        for c in range(count - 1, 0, -1):
            part = [b for j, b in enumerate(group) if (c >> (len(group) - 1 - j)) & 1]
            mask = sum(1 << b for b in part)
            message = chunks[c]
            if len(part) == 1 and part[0] in over_factor:
                trade_send, trade_keep = jnp.split(trade_keep + trade_more, 2, 0)[::-1]
                if i > 0 and message.shape[2] == LANES:
                    cut = trade_send.shape[0] * trade_send.shape[1]
                    message = jnp.concatenate(
                        [trade_send.reshape(cut, LANES), message.reshape(-1, LANES)], 0
                    )
                    message = exchange(message, mask)
                    trade_more = message[:cut].reshape(trade_send.shape)
                    message = message[cut:].reshape(chunks[c].shape)
                else:
                    trade_more = exchange(trade_send, mask)
                    message = exchange(message, mask)
            else:
                message = exchange(message, mask)
            pieces.append(message)
        if i == 0:
            next_count = 1 << len(groups[1])
            chunk = shape(HIGH // count // next_count, 3 * BUCKETS, LANES)
            chunks = call(
                functools.partial(middle_kernel, count=count),
                (chunk,) * next_count,
                [VMEM] * count,
                (VMEM,) * next_count,
                "middle",
                flops=10**6,
            )(*pieces)
        elif i + 1 < len(groups):
            keep = sum(pieces[1:], pieces[0])
    return call(
        functools.partial(finish_kernel, scale=1.0 / trades_total**0.5),
        (
            shape(SCEN),
            shape(SCEN, trade_rows // factor_size),
            shape(SCEN, BUCKETS, NODES // devices),
        ),
        [VMEM] * (4 + len(pieces)),
        (SMEM, VMEM, VMEM),
        "finish",
        flops=10**6,
    )(mix, capital, trade_keep[0], trade_more[0], *[p[0] for p in pieces])


def solution(mesh):
    sizes = dict(mesh.shape)
    return jax.shard_map(
        functools.partial(local, trade_size=sizes["trade"], factor_size=sizes["factor"]),
        mesh=mesh,
        in_specs=(P("trade", "factor"), P("trade"), P("trade"), P(), P(), P()),
        out_specs=(P(), P(None, ("trade", "factor")), P(None, None, ("trade", "factor"))),
        check_vma=False,
    )
```
